512 devices in a mesh: rows: 8 (over y, core), tp: 64 (over z, x).
Axes of the slice: x: 4, y: 4, z: 16, core: 2. Of those that a mesh axis runs over, the one named last changes fastest.
Arguments:
- hidden: bfloat16 [2, 1024, 16384], P(None, ('rows', 'tp')), may hold values from -6 to 6
- adapter_ids: int32 [1024, 1], P('rows'), may hold values from 0 to 63; in each aligned block of 128 rows (0 to 127, 128 to 255, ...) at most 8 rows name the same one
- key_weight: bfloat16 [16384, 1024], P('tp'), may hold values from -0.046875 to 0.046875
- value_weight: bfloat16 [16384, 1024], P('tp'), may hold values from -0.046875 to 0.046875
- adapter_down: bfloat16 [16384, 4096], P('rows', 'tp'), may hold values from -0.046875 to 0.046875
- adapter_up: bfloat16 [64, 64, 1024], P('tp'), may hold values from -0.75 to 0.75
Outputs:
- key_out: bfloat16 [2, 1024, 1024], P(None, ('rows', 'tp'))
- value_out: bfloat16 [2, 1024, 1024], P(None, ('rows', 'tp'))
The draws below stay inside these ranges and needn't reach their ends.
Inputs may be any that keep to these rules, and one draw needn't show every extreme that they name: `adapter_ids`: in each aligned block of 128 rows no adapter is named by more than 8 rows, a bound that some block reaches.
All inputs are finite; a program needn't handle non-finite values.
Results may differ from the reference program's by a relative error of at most 0.0085.
Values may be sent and summed in bfloat16 or wider, within the bound.
A program may use at most 64 MiB of HBM per device.

```python
import math
import jax
import jax.numpy as jnp
import numpy as np
from jax import lax

D = 16384
KVD = 1024
RANK = 64
STEPS = 2
ADAPTERS = 64
GROUP_ROWS = 128
ROWS = 1024
LOAD = 8


def block_scale(key, extent, split, smallest, largest):
    def one(dim, parts):
        heights = jax.random.uniform(jax.random.fold_in(jax.random.fold_in(key, 6), dim), (parts,), jnp.float32, smallest / len(split), largest / len(split))
        return jnp.repeat(jnp.exp(heights), extent[dim] // parts).reshape((-1,) + (1,) * (len(extent) - dim - 1))

    level = one(*split[0])
    for cut in split[1:]:
        level = level * one(*cut)
    return level


def shared_out(rng, own, number, rows, amount, top, reach, skew):
    ranking = jax.random.permutation(rng, amount)
    crowded, ordinary = load_shares(amount, rows * top, reach, skew, True), load_shares(amount, rows * top, reach, skew, False)
    places = jnp.arange(amount)

    def named(sizes, offset_by):
        used = int((sizes > 0).sum())
        fixed = max(1, used // 4)
        shifted = fixed + (places - fixed + offset_by * (used - fixed)) % max(1, amount - fixed)
        return jnp.zeros((amount,), jnp.int32).at[ranking[jnp.where(places < fixed, places, shifted)]].set(jnp.asarray(sizes, jnp.int32))

    sizes = jnp.where(number % 4 == 0, named(crowded, number // 4), named(ordinary, number - number // 4 - 1))
    mixed = jax.random.permutation(jax.random.fold_in(own, 3), amount)
    donor, sink = mixed[0:amount // 2 * 2:2], mixed[1:amount // 2 * 2:2]
    margin = jnp.minimum(sizes[donor] - 1, reach - sizes[sink]) // 2
    margin = jnp.where((donor == ranking[0]) | (sink == ranking[0]) | (sizes[sink] == 0), 0, jnp.maximum(margin, 0))
    shifted = jax.random.randint(jax.random.fold_in(own, 4), (amount // 2,), 0, 1 << 20) % (margin + 1)
    sizes = sizes.at[donor].add(-shifted).at[sink].add(shifted)
    members = jnp.searchsorted(jnp.cumsum(sizes), jnp.arange(rows * top), side="right").astype(jnp.int32)
    grid = members.reshape(top, rows).T
    grid = grid[jax.random.permutation(jax.random.fold_in(own, 1), rows)]
    offset_by = jax.random.randint(jax.random.fold_in(own, 2), (rows, 1), 0, top)
    return jnp.take_along_axis(grid, (jnp.arange(top)[None, :] + offset_by) % top, axis=1)


def load_shares(number_of, total, limit, slope, full):
    weights = [(1 << 20) // math.isqrt(standing ** slope) + 1 for standing in range(1, number_of + 1)]
    largest = limit if full else min(limit, max(-(-total // number_of), total * weights[0] // sum(weights)))
    least = 1 if total - largest >= number_of - 1 else 0
    holding, surplus = [largest] + [least] * (number_of - 1), total - largest - least * (number_of - 1)
    while surplus > 0:
        movable = [i for i in range(1, number_of) if holding[i] < largest] or [i for i in range(1, number_of) if holding[i] < limit]
        pool, budget = sum([weights[i] for i in movable]), surplus
        for i in movable:
            extra = min(limit - holding[i], max(1, budget * weights[i] // pool), surplus)
            holding[i] = holding[i] + extra
            surplus = surplus - extra
    return np.array(holding)


def noise(rng, shape, spread, most, shards=(), kind=jnp.bfloat16):
    entries = spread * jax.random.normal(rng, shape, jnp.float32)
    if shards:
        entries = entries * block_scale(rng, shape, shards, -0.22, 0.18)
    return jnp.clip(entries, -most, most).astype(kind)


def setup_inputs(seed: int = 0) -> dict:
    arg_keys = jax.random.split(jax.random.key(seed), 7)
    hidden = noise(arg_keys[0], (STEPS, ROWS, D), 1.0, 6.0, ((1, 512),))
    adapter_ids_keys = jax.random.split(jax.random.fold_in(arg_keys[1], 1), ROWS // GROUP_ROWS)
    adapter_ids_turns = jax.random.permutation(jax.random.fold_in(arg_keys[1], 3), ROWS // GROUP_ROWS)
    adapter_ids = jax.vmap(lambda own, number: shared_out(jax.random.fold_in(arg_keys[1], 2), own, number, GROUP_ROWS, ADAPTERS, 1, LOAD, 2))(adapter_ids_keys, adapter_ids_turns).reshape((ROWS, 1))
    key_weight = noise(arg_keys[2], (D, KVD), D ** -0.5, 0.046875, ((0, 64),))
    value_weight = noise(arg_keys[3], (D, KVD), D ** -0.5, 0.046875, ((0, 64),))
    adapter_down = noise(arg_keys[4], (D, ADAPTERS * RANK), D ** -0.5, 0.046875, ((0, 8), (1, 64)))
    adapter_up = noise(arg_keys[5], (ADAPTERS, RANK, KVD), RANK ** -0.5, 0.75, ((0, 64),))
    return dict(hidden=hidden, adapter_ids=adapter_ids, key_weight=key_weight, value_weight=value_weight, adapter_down=adapter_down, adapter_up=adapter_up)


def reference(hidden, adapter_ids, key_weight, value_weight, adapter_down, adapter_up):
    row_ids = adapter_ids[:, 0]
    onehot = (row_ids[:, None] == jnp.arange(ADAPTERS, dtype=jnp.int32)[None, :]).astype(jnp.float32)
    up_flat = adapter_up.astype(jnp.float32).reshape(ADAPTERS * RANK, KVD)
    key_list = []
    value_list = []
    for step in range(STEPS):
        tokens_now = hidden[step]
        key_rows = jnp.dot(tokens_now, key_weight, preferred_element_type=jnp.float32).astype(jnp.bfloat16)
        all_shrink = jnp.dot(tokens_now, adapter_down, preferred_element_type=jnp.float32)
        all_shrink = all_shrink.reshape(ROWS, ADAPTERS, RANK)
        shrink = jnp.sum(all_shrink * onehot[:, :, None], axis=1).astype(jnp.bfloat16)
        placed = (shrink.astype(jnp.float32)[:, None, :] * onehot[:, :, None]).reshape(ROWS, ADAPTERS * RANK)
        lowrank = jnp.dot(placed, up_flat, precision=lax.Precision.HIGHEST)
        base_values = jnp.dot(tokens_now, value_weight, preferred_element_type=jnp.float32)
        key_list.append(key_rows)
        value_list.append((base_values + lowrank).astype(jnp.bfloat16))
    return jnp.stack(key_list), jnp.stack(value_list)
```

```python
import functools

import jax
import jax.numpy as jnp
from jax import lax
from jax.experimental import pallas as pl
from jax.experimental.pallas import tpu as pltpu
from jax.sharding import PartitionSpec as P

MESH = pl.DeviceIdType.MESH
BF16 = jnp.bfloat16
F32 = jnp.float32
CORES = 2
SLOTS = 8
RANK = 64


def dot(a, b):
    return jnp.dot(a, b, preferred_element_type=F32)


def dot_t(a, b):
    return lax.dot_general(a, b, (((1,), (1,)), ((), ())), preferred_element_type=F32)


def log2(n):
    return n.bit_length() - 1


def kernel(
    nr, nz, nx,
    x_ref, idr_ref, idc_ref, wk_ref, wv_ref, dn_ref, up_ref,
    ko_ref, vo_ref,
    xg, wkg, wvg, ug, dsp, dg, xm, ss, sr, sh, ks, kr, vs, vr, og,
    loc, xz_s, xz_r, xx_s, xx_r, wk_s, wk_r, wv_s, wv_r, up_s, up_r,
    dr_s, dr_r, dz_s, dz_r, dy_s, dy_r, dc_s, dc_r,
    s_s, s_r, sh_s, sh_r, k_s, k_r, v_s, v_r, o_s, o_r,
):
    ny = nr // CORES
    lbs = x_ref.shape[1] // 4
    width = wkg.shape[2]
    fe = dn_ref.shape[3]
    rows = nz * nx * 4
    i = lax.axis_index("rows")
    p = lax.axis_index("tp")
    y, c = i // CORES, i % CORES
    z, x = p // nx, p % nx

    def at_z(k):
        return lax.rem(z + k, nz)

    def at_x(k):
        return lax.rem(x + k, nx)

    def z_dev(zz):
        return (i, zz * nx + x)

    def x_dev(xx):
        return (i, z * nx + xx)

    def r_dev(ii):
        return (ii, p)

    def send(src, dst, ss_, rs_, dev):
        return pltpu.make_async_remote_copy(
            src_ref=src, dst_ref=dst, send_sem=ss_, recv_sem=rs_, device_id=dev, device_id_type=MESH
        )

    barrier = pltpu.get_barrier_semaphore()
    for k in range(1, nr):
        pl.semaphore_signal(barrier, inc=1, device_id=r_dev(lax.rem(i + k, nr)), device_id_type=MESH)
    for k in range(1, nx):
        pl.semaphore_signal(barrier, inc=1, device_id=x_dev(at_x(k)), device_id_type=MESH)

    def greet(k, carry):
        pl.semaphore_signal(barrier, inc=1, device_id=z_dev(at_z(k)), device_id_type=MESH)
        return carry

    lax.fori_loop(1, nz, greet, 0)
    pl.semaphore_wait(barrier, nr + nx + nz - 3)

    def xz_copy(k, to):
        return send(x_ref.at[to], xg.at[x, z], xz_s.at[k], xz_r.at[k], z_dev(to))

    lax.fori_loop(1, nz, lambda k, t: (xz_copy(k, at_z(k)).start(), t)[1], 0)
    x_own = pltpu.make_async_copy(x_ref.at[z], xg.at[x, z], loc.at[0])
    x_own.start()

    def dr_copy(k):
        to = lax.rem(i + k, nr)
        return send(dn_ref.at[to], dsp.at[pl.ds(2 * i, 2)], dr_s.at[k], dr_r.at[k], r_dev(to))

    for k in range(1, nr):
        dr_copy(k).start()
    d_own = pltpu.make_async_copy(dn_ref.at[i], dsp.at[pl.ds(2 * i, 2)], loc.at[1])
    d_own.start()

    def col(xx):
        return pl.ds(pl.multiple_of(xx * width, width), width)

    def w_copies(k):
        to = at_x(k)
        return (
            send(wk_ref.at[:, col(to)], wkg.at[x], wk_s.at[k], wk_r.at[k], x_dev(to)),
            send(wv_ref.at[:, col(to)], wvg.at[x], wv_s.at[k], wv_r.at[k], x_dev(to)),
            send(up_ref.at[:, col(to)], ug.at[x], up_s.at[k], up_r.at[k], x_dev(to)),
        )

    for k in range(1, nx):
        for one in w_copies(k):
            one.start()
    w_own = (
        pltpu.make_async_copy(wk_ref.at[:, col(x)], wkg.at[x], loc.at[2]),
        pltpu.make_async_copy(wv_ref.at[:, col(x)], wvg.at[x], loc.at[3]),
        pltpu.make_async_copy(up_ref.at[:, col(x)], ug.at[x], loc.at[4]),
    )
    for one in w_own:
        one.start()

    for k in range(1, nr):
        dr_copy(k).wait_recv()
    d_own.wait()

    def dz_copy(k, to):
        return send(dsp.at[to], dg.at[i, z], dz_s.at[k], dz_r.at[k], z_dev(to))

    lax.fori_loop(1, nz, lambda k, t: (dz_copy(k, at_z(k)).start(), t)[1], 0)
    e_own = pltpu.make_async_copy(dsp.at[z], dg.at[i, z], loc.at[5])
    e_own.start()

    lax.fori_loop(1, nz, lambda k, t: (xz_copy(k, at_z(k)).wait_recv(), t)[1], 0)
    x_own.wait()

    def xx_copy(k):
        return send(xg.at[x], xg.at[x], xx_s.at[k], xx_r.at[k], x_dev(at_x(k)))

    for k in range(1, nx):
        xx_copy(k).start()

    bits_x, bits_lb = log2(nx), log2(lbs)
    idr, idc = idr_ref[...], idc_ref[...]
    rho_r = lax.broadcasted_iota(jnp.int32, (rows, rows), 1)
    rho_c = lax.broadcasted_iota(jnp.int32, (rows, rows), 0)
    same = (idr == idc) & (((rho_r ^ rho_c) & 2) == 0)
    slot_r = jnp.sum((same & (rho_c < rho_r)).astype(F32), axis=0, keepdims=True).astype(jnp.int32)
    slot_c = jnp.sum((same & (rho_r < rho_c)).astype(F32), axis=1, keepdims=True).astype(jnp.int32)
    slots = 2 * nz * SLOTS
    sig = lax.broadcasted_iota(jnp.int32, (slots, rows), 0)
    rho = lax.broadcasted_iota(jnp.int32, (slots, rows), 1)
    half = nz * SLOTS
    t_sig = (sig >= half).astype(jnp.int32)
    za_sig = (sig & (half - 1)) >> 3
    gather = (
        (idr == za_sig * nx + x) & (slot_r == (sig & (SLOTS - 1))) & (((rho >> 1) & 1) == t_sig)
    ).astype(F32).astype(BF16)

    block = 2 * nx * 4 * lbs
    o = lax.broadcasted_iota(jnp.int32, (block, block), 0)
    n = lax.broadcasted_iota(jnp.int32, (block, block), 1)
    r_o = o & 3
    x_o = (o >> 2) & (nx - 1)
    z_o = (o >> (2 + bits_x)) & 1
    l_o = o >> (3 + bits_x)
    perm = (n == ((((x_o * 2 + z_o) * 4 + r_o) << bits_lb) + l_o)).astype(F32).astype(BF16)

    def dy_copy(j, zz):
        to = lax.rem(y + j, ny) * CORES + c
        return send(dg.at[i, zz], dg.at[i, zz], dy_s.at[j], dy_r.at[j], r_dev(to))

    def forward(k, t):
        zz = lax.rem(z + nz - k, nz)
        dz_copy(k, zz).wait_recv()
        for j in range(1, ny):
            dy_copy(j, zz).start()
        return t

    e_own.wait()
    for j in range(1, ny):
        dy_copy(j, z).start()
    lax.fori_loop(1, nz // 2, forward, 0)

    for k in range(1, nx):
        xx_copy(k).wait_recv()
    zb = nz // 2
    wide = jnp.concatenate(
        [xg[:, 2 * b:2 * b + 2].reshape(block, 128) for b in range(zb)], axis=1
    )
    turned = dot(perm, wide).astype(BF16)
    part = 8 * nx
    for b in range(zb):
        for lb in range(lbs):
            xm[b * part:(b + 1) * part, lb * 128:(lb + 1) * 128] = turned[
                lb * part:(lb + 1) * part, b * 128:(b + 1) * 128
            ]
    for k in range(1, nx):
        for one in w_copies(k):
            one.wait_recv()
    for one in w_own:
        one.wait()
    per = rows // nz
    kp = dot(xm[...], wkg[...].reshape(nx * wkg.shape[1], width))
    ks[...] = kp.astype(BF16).reshape(nz, per, width)

    lax.fori_loop(nz // 2, nz, forward, 0)

    def k_copy(k, to):
        return send(ks.at[to], kr.at[z], k_s.at[k], k_r.at[k], z_dev(to))

    lax.fori_loop(1, nz, lambda k, t: (k_copy(k, at_z(k)).start(), t)[1], 0)
    kr[z] = ks[z]

    def dc_copy(j):
        e = lax.rem(y + ny - j, ny) * CORES + c
        return send(dg.at[e], dg.at[e], dc_s.at[j], dc_r.at[j], r_dev(y * CORES + 1 - c))

    def dy_whole(j):
        e = lax.rem(y + ny - j, ny) * CORES + c
        return send(dg.at[e], dg.at[e], dy_s.at[j], dy_r.at[j], r_dev(lax.rem(y + j, ny) * CORES + c))

    dc_copy(0).start()
    vp = dot(xm[...], wvg[...].reshape(nx * wvg.shape[1], width))
    picked = dot(gather, xm[...]).astype(BF16)
    for j in range(1, ny):
        dy_whole(j).wait_recv()
        dc_copy(j).start()
    for j in range(ny):
        dc_copy(j).wait_recv()

    cols = nz * RANK
    acc = jnp.zeros((slots, cols), F32)
    for e in range(nr):
        acc = acc + dot_t(picked[:, e * fe:(e + 1) * fe], dg[e].reshape(cols, fe))
    for a in range(nz):
        first = acc[a * SLOTS:(a + 1) * SLOTS, a * RANK:(a + 1) * RANK]
        second = acc[half + a * SLOTS:half + (a + 1) * SLOTS, a * RANK:(a + 1) * RANK]
        ss[a] = jnp.concatenate([first, second], axis=1)

    def s_copy(k, to):
        return send(ss.at[to], sr.at[z], s_s.at[k], s_r.at[k], z_dev(to))

    lax.fori_loop(1, nz, lambda k, t: (s_copy(k, at_z(k)).start(), t)[1], 0)
    sr[z] = ss[z]
    lax.fori_loop(1, nz, lambda k, t: (s_copy(k, at_z(k)).wait_recv(), t)[1], 0)
    sh[x] = jnp.sum(sr[...], axis=0).astype(BF16).astype(F32)

    def sh_copy(k):
        return send(sh.at[x], sh.at[x], sh_s.at[k], sh_r.at[k], x_dev(at_x(k)))

    for k in range(1, nx):
        sh_copy(k).start()
    spot = lax.broadcasted_iota(jnp.int32, (rows, nx * SLOTS), 1)
    place = (
        (idc == z * nx + (spot >> 3)) & (slot_c == (spot & (SLOTS - 1)))
    ).astype(F32).astype(BF16)
    lane = lax.broadcasted_iota(jnp.int32, (rows, 2 * RANK), 1)
    rho_l = lax.broadcasted_iota(jnp.int32, (rows, 2 * RANK), 0)
    mine = ((rho_l >> 1) & 1) == (lane >= RANK).astype(jnp.int32)
    for k in range(1, nx):
        sh_copy(k).wait_recv()
    low = jnp.where(mine, dot(place, sh[...].reshape(nx * SLOTS, 2 * RANK).astype(BF16)), 0.0)
    for xa in range(nx):
        low_a = jnp.where(idc == z * nx + xa, low, 0.0).astype(BF16)
        vp = vp + dot(low_a, jnp.concatenate([ug[xa], ug[xa]], axis=0))
    vs[...] = vp.astype(BF16).reshape(nz, per, width)

    def v_copy(k, to):
        return send(vs.at[to], vr.at[z], v_s.at[k], v_r.at[k], z_dev(to))

    lax.fori_loop(1, nz, lambda k, t: (v_copy(k, at_z(k)).start(), t)[1], 0)
    vr[z] = vs[z]
    lax.fori_loop(1, nz, lambda k, t: (k_copy(k, at_z(k)).wait_recv(), t)[1], 0)
    k_sum = jnp.sum(kr[...].astype(F32), axis=0)
    lax.fori_loop(1, nz, lambda k, t: (v_copy(k, at_z(k)).wait_recv(), t)[1], 0)
    v_sum = jnp.sum(vr[...].astype(F32), axis=0)
    og[x] = jnp.concatenate([k_sum, v_sum], axis=1).astype(BF16)

    def o_copy(k):
        return send(og.at[x], og.at[x], o_s.at[k], o_r.at[k], x_dev(at_x(k)))

    for k in range(1, nx):
        o_copy(k).start()

    def left(k, t):
        xz_copy(k, at_z(k)).wait_send()
        dz_copy(k, at_z(k)).wait_send()
        s_copy(k, at_z(k)).wait_send()
        k_copy(k, at_z(k)).wait_send()
        v_copy(k, at_z(k)).wait_send()
        return t

    lax.fori_loop(1, nz, left, 0)
    for k in range(1, nr):
        dr_copy(k).wait_send()
    for k in range(1, nx):
        for one in w_copies(k):
            one.wait_send()
        xx_copy(k).wait_send()
        sh_copy(k).wait_send()
    for j in range(1, ny):
        dy_whole(j).wait_send()
    for j in range(ny):
        dc_copy(j).wait_send()

    for k in range(1, nx):
        o_copy(k).wait_recv()
    want = lax.broadcasted_iota(jnp.int32, (8, per), 1) == (
        lax.broadcasted_iota(jnp.int32, (8, per), 0) + 4 * x
    )
    want = want.astype(F32).astype(BF16)
    for xx in range(nx):
        mine4 = dot(want, og[xx])[:4].astype(BF16)
        ko_ref[:, xx * width:(xx + 1) * width] = mine4[:, :width]
        vo_ref[:, xx * width:(xx + 1) * width] = mine4[:, width:]
    for k in range(1, nx):
        o_copy(k).wait_send()


def shards(nr, nz, nx, hidden, adapter_ids, key_weight, value_weight, adapter_down, adapter_up):
    steps, own, wide = hidden.shape
    width = key_weight.shape[1] // nx
    deep = key_weight.shape[0]
    fz = wide // nz
    lbs = fz // 128
    fe = fz // nr
    rows = nz * nx * 4
    xz = hidden.reshape(4, nz, lbs, 128).transpose(1, 0, 2, 3).reshape(nz, 4 * lbs, 128)
    ids = jnp.broadcast_to(adapter_ids.reshape(nz * nx, 1, own), (nz * nx, steps, own))
    dn = adapter_down.reshape(2, nr, fe, RANK).transpose(1, 0, 3, 2)
    any_, vmem = pl.BlockSpec(memory_space=pl.ANY), pl.BlockSpec(memory_space=pltpu.VMEM)
    dma = pltpu.SemaphoreType.DMA
    per = rows // nz
    key_out, value_out = pl.pallas_call(
        functools.partial(kernel, nr, nz, nx),
        out_shape=[jax.ShapeDtypeStruct((4, nx * width), BF16)] * 2,
        in_specs=[any_, vmem, vmem, any_, any_, any_, any_],
        out_specs=[vmem, vmem],
        scratch_shapes=[
            pltpu.VMEM((nx, nz, 4 * lbs, 128), BF16),
            pltpu.VMEM((nx, deep, width), BF16),
            pltpu.VMEM((nx, deep, width), BF16),
            pltpu.VMEM((nx, RANK, width), BF16),
            pltpu.VMEM((nz, RANK, fe), BF16),
            pltpu.VMEM((nr, nz, RANK, fe), BF16),
            pltpu.VMEM((rows, fz), BF16),
            pltpu.VMEM((nz, SLOTS, 2 * RANK), F32),
            pltpu.VMEM((nz, SLOTS, 2 * RANK), F32),
            pltpu.VMEM((nx, SLOTS, 2 * RANK), F32),
            pltpu.VMEM((nz, per, width), BF16),
            pltpu.VMEM((nz, per, width), BF16),
            pltpu.VMEM((nz, per, width), BF16),
            pltpu.VMEM((nz, per, width), BF16),
            pltpu.VMEM((nx, per, 2 * width), BF16),
            dma((6,)),
            dma((nz,)), dma((nz,)), dma((nx,)), dma((nx,)),
            dma((nx,)), dma((nx,)), dma((nx,)), dma((nx,)), dma((nx,)), dma((nx,)),
            dma((nr,)), dma((nr,)), dma((nz,)), dma((nz,)),
            dma((nr,)), dma((nr,)), dma((nr,)), dma((nr,)),
            dma((nz,)), dma((nz,)), dma((nx,)), dma((nx,)),
            dma((nz,)), dma((nz,)), dma((nz,)), dma((nz,)), dma((nx,)), dma((nx,)),
        ],
        compiler_params=pltpu.CompilerParams(
            collective_id=0, has_side_effects=True, vmem_limit_bytes=32 * 1024 * 1024
        ),
        cost_estimate=pl.CostEstimate(flops=2_000_000_000, bytes_accessed=4_000_000, transcendentals=0),
    )(xz, ids.reshape(1, rows), ids.reshape(rows, 1), key_weight, value_weight, dn, adapter_up[0])
    return key_out.reshape(steps, own, -1), value_out.reshape(steps, own, -1)


def solution(mesh):
    nr, tp = mesh.shape["rows"], mesh.shape["tp"]
    nx = 4 if tp >= 64 else 2
    placed = (
        P(None, ("rows", "tp"), None),
        P("rows", None),
        P("tp", None),
        P("tp", None),
        P("rows", "tp"),
        P("tp", None, None),
    )
    return jax.shard_map(
        functools.partial(shards, nr, tp // nx, nx),
        mesh=mesh,
        in_specs=placed,
        out_specs=(P(None, ("rows", "tp"), None), P(None, ("rows", "tp"), None)),
        check_vma=False,
    )
```

```python
import functools

import jax
import jax.numpy as jnp
from jax import lax
from jax.experimental import pallas as pl
from jax.experimental.pallas import tpu as pltpu
from jax.sharding import PartitionSpec as P

MESH = pl.DeviceIdType.MESH
BF16 = jnp.bfloat16
F32 = jnp.float32
CORES = 2
SLOTS = 8
RANK = 64


def dot(a, b):
    return jnp.dot(a, b, preferred_element_type=F32)


def dot_t(a, b):
    return lax.dot_general(a, b, (((1,), (1,)), ((), ())), preferred_element_type=F32)


def log2(n):
    return n.bit_length() - 1


TURNS = {16: (8, 7, 1, 0, 9, 6, 2, 15, 10, 5, 3, 14, 11, 4, 12, 13), 4: (2, 0, 1, 3)}


def kernel(
    nr, nz, nx, ng,
    x_ref, id_ref, wk_ref, wv_ref, dn_ref, up_ref,
    ko_ref, vo_ref,
    xg, wkg, wvg, ug, dsp, dg, xm, ss, sr, sh, ks, kr, vs, vr,
    loc, xz_s, xz_r, xx_s, xx_r, wk_s, wk_r, wv_s, wv_r, wkc_s, wkc_r, wvc_s, wvc_r, up_s, up_r, upc_s, upc_r,
    dr_s, dr_r, dz_s, dz_r, dy_s, dy_r, dc_s, dc_r,
    s_s, s_r, sh_s, sh_r, k_s, k_r, v_s, v_r,
):
    ny = nr // CORES
    qg = nz // ng
    lbs = x_ref.shape[1] // 4
    width = wkg.shape[2]
    lbo = width // 128
    fe = dn_ref.shape[3]
    rows = nz * nx * 4
    i = lax.axis_index("rows")
    p = lax.axis_index("tp")
    y, c = i // CORES, i % CORES
    z, x = p // nx, p % nx
    far = nz // 2

    def step(q):
        return far + (1 - 2 * (q % 2)) * ((q + 1) // 2)

    def to_z(q):
        return (z + step(q)) % nz

    hops = TURNS[nz]

    def at_x(k):
        return (x + k) % nx

    def z_dev(zz):
        return (i, zz * nx + x)

    def x_dev(xx):
        return (i, z * nx + xx)

    def r_dev(ii):
        return (ii, p)

    other = r_dev(y * CORES + 1 - c)

    def send(src, dst, ss_, rs_, dev):
        return pltpu.make_async_remote_copy(
            src_ref=src, dst_ref=dst, send_sem=ss_, recv_sem=rs_, device_id=dev, device_id_type=MESH
        )

    def turns(body):
        def one(q, t):
            body(q)
            return t

        lax.fori_loop(0, nz - 1, one, 0)

    barrier = pltpu.get_barrier_semaphore()
    turns(lambda q: pl.semaphore_signal(barrier, inc=1, device_id=z_dev(to_z(q)), device_id_type=MESH))
    for k in range(1, nr):
        pl.semaphore_signal(barrier, inc=1, device_id=r_dev((i + k) % nr), device_id_type=MESH)
    for k in range(1, nx):
        pl.semaphore_signal(barrier, inc=1, device_id=x_dev(at_x(k)), device_id_type=MESH)

    x_own = pltpu.make_async_copy(x_ref.at[z], xg.at[x, z], loc.at[0])
    d_own = pltpu.make_async_copy(dn_ref.at[i], dsp.at[pl.ds(2 * i, 2)], loc.at[1])
    w_own = (
        pltpu.make_async_copy(wk_ref, wkg.at[x], loc.at[2]),
        pltpu.make_async_copy(wv_ref, wvg.at[x], loc.at[3]),
        pltpu.make_async_copy(up_ref, ug.at[x], loc.at[4]),
    )
    for one in (x_own, d_own) + w_own:
        one.start()

    pl.semaphore_wait(barrier, nr + nx + nz - 3)

    def xz_copy(q):
        return send(x_ref.at[to_z(q)], xg.at[x, z], xz_s.at[q], xz_r.at[q], z_dev(to_z(q)))

    def dr_copy(k):
        to = (i + k) % nr
        return send(dn_ref.at[to], dsp.at[pl.ds(2 * i, 2)], dr_s.at[k], dr_r.at[k], r_dev(to))

    for k in range(1, nr):
        dr_copy(k).start()
    turns(lambda q: xz_copy(q).start())

    deep = wk_ref.shape[0]

    def share(n):
        return pl.ds(pl.multiple_of(c * (n // CORES), n // CORES), n // CORES)

    def wk_copy(k):
        some = share(deep)
        return send(wk_ref.at[some], wkg.at[x, some], wk_s.at[k], wk_r.at[k], x_dev(at_x(k)))

    def wv_copy(k):
        some = share(deep)
        return send(wv_ref.at[some], wvg.at[x, some], wv_s.at[k], wv_r.at[k], x_dev(at_x(k)))

    def up_copy(k):
        some = share(RANK)
        return send(up_ref.at[some], ug.at[x, some], up_s.at[k], up_r.at[k], x_dev(at_x(k)))

    def pass_on(ref, n, s_sem, r_sem, k):
        xx, some = (x + nx - k) % nx, share(n)
        return send(ref.at[xx, some], ref.at[xx, some], s_sem.at[k], r_sem.at[k], other)

    def wkc_copy(k):
        return pass_on(wkg, deep, wkc_s, wkc_r, k)

    def wvc_copy(k):
        return pass_on(wvg, deep, wvc_s, wvc_r, k)

    def upc_copy(k):
        return pass_on(ug, RANK, upc_s, upc_r, k)

    for k in range(1, nx):
        wk_copy(k).start()

    group = rows // 2
    ids = jnp.broadcast_to(id_ref[...].astype(F32).astype(BF16), (8, group))
    r_a = lax.broadcasted_iota(jnp.int32, (group, rows), 0)
    n_a = lax.broadcasted_iota(jnp.int32, (group, rows), 1)
    idr = dot(ids, (r_a == (n_a >> 2) * 2 + (n_a & 1)).astype(F32).astype(BF16))[:1].astype(jnp.int32)
    r_b = lax.broadcasted_iota(jnp.int32, (rows, group), 1)
    n_b = lax.broadcasted_iota(jnp.int32, (rows, group), 0)
    idc = dot_t((r_b == (n_b >> 2) * 2 + (n_b & 1)).astype(F32).astype(BF16), ids)[:, :1].astype(jnp.int32)

    bits_x, bits_lb = log2(nx), log2(lbs)
    rho_r = lax.broadcasted_iota(jnp.int32, (rows, rows), 1)
    rho_c = lax.broadcasted_iota(jnp.int32, (rows, rows), 0)
    same = (idr == idc) & (((rho_r ^ rho_c) & 2) == 0)
    slot_r = jnp.sum((same & (rho_c < rho_r)).astype(F32), axis=0, keepdims=True).astype(jnp.int32)
    slot_c = jnp.sum((same & (rho_r < rho_c)).astype(F32), axis=1, keepdims=True).astype(jnp.int32)
    half = qg * SLOTS
    slots = 2 * nz * SLOTS
    sig = lax.broadcasted_iota(jnp.int32, (slots, rows), 0)
    rho = lax.broadcasted_iota(jnp.int32, (slots, rows), 1)
    t_sig = (sig >> log2(half)) & 1
    col_sig = lax.broadcasted_iota(jnp.int32, (slots, 1), 0)
    q_sig = (col_sig >> log2(2 * half)) * qg + ((col_sig & (half - 1)) >> 3)
    za_sig = jnp.zeros((slots, 1), jnp.int32)
    for q in range(nz):
        za_sig = jnp.where(q_sig == q, (z + nz - hops[q]) % nz, za_sig)
    gather = (
        (idr == za_sig * nx + x) & (slot_r == (sig & (SLOTS - 1))) & (((rho >> 1) & 1) == t_sig)
    ).astype(F32).astype(BF16)
    spot = lax.broadcasted_iota(jnp.int32, (rows, nx * SLOTS), 1)
    place = (
        (idc == z * nx + (spot >> 3)) & (slot_c == (spot & (SLOTS - 1)))
    ).astype(F32).astype(BF16)

    block = 2 * nx * 4 * lbs
    o = lax.broadcasted_iota(jnp.int32, (block, block), 0)
    n = lax.broadcasted_iota(jnp.int32, (block, block), 1)
    r_o = o & 3
    x_o = (o >> 2) & (nx - 1)
    z_o = (o >> (2 + bits_x)) & 1
    l_o = o >> (3 + bits_x)
    perm = (n == ((((x_o * 2 + z_o) * 4 + r_o) << bits_lb) + l_o)).astype(F32).astype(BF16)

    tail = nz * 4
    o_own = lax.broadcasted_iota(jnp.int32, (tail, rows), 0)
    n_own = lax.broadcasted_iota(jnp.int32, (tail, rows), 1)
    own = (n_own == (o_own >> 2) * (4 * nx) + 4 * x + (o_own & 3)).astype(F32).astype(BF16)
    place = dot(own, place)
    big = tail * lbo
    o_out = lax.broadcasted_iota(jnp.int32, (big, big), 0)
    n_out = lax.broadcasted_iota(jnp.int32, (big, big), 1)
    spread = (
        n_out == (o_out & (lbo - 1)) * tail + (o_out >> log2(lbo))
    ).astype(F32).astype(BF16)

    def parcels(part):
        tall = jnp.concatenate([part[:, lb * 128:(lb + 1) * 128] for lb in range(lbo)], axis=0)
        return dot(spread, tall).astype(BF16).reshape(nz, 4 * lbo, 128)

    for k in range(1, nr):
        dr_copy(k).wait_recv()
    d_own.wait()

    def dz_copy(q):
        to = (z + hops[q]) % nz
        return send(dsp.at[to], dg.at[i, q], dz_s.at[q], dz_r.at[q], z_dev(to))

    def over_z(g):
        if g > 1:
            for q in range((g - 2) * qg, (g - 1) * qg):
                if hops[q]:
                    dz_copy(q).wait_send()
        for q in range(g * qg, (g + 1) * qg):
            if hops[q]:
                dz_copy(q).start()

    over_z(0)
    over_z(1)
    e_own = pltpu.make_async_copy(dsp.at[z], dg.at[i, hops.index(0)], loc.at[5])
    e_own.start()

    turns(lambda q: xz_copy(q).wait_recv())
    x_own.wait()

    def xx_copy(k):
        return send(xg.at[x], xg.at[x], xx_s.at[k], xx_r.at[k], x_dev(at_x(k)))

    for k in range(1, nx):
        xx_copy(k).start()

    def dy_copy(j, g):
        some = pl.ds(g * qg, qg)
        to = ((y + j) % ny) * CORES + c
        return send(dg.at[i, some], dg.at[i, some], dy_s.at[j, g], dy_r.at[j, g], r_dev(to))

    def dc_copy(j, g):
        some = pl.ds(g * qg, qg)
        e = ((y + ny - j) % ny) * CORES + c
        return send(dg.at[e, some], dg.at[e, some], dc_s.at[j, g], dc_r.at[j, g], other)

    def over_y(g):
        for q in range(g * qg, (g + 1) * qg):
            if hops[q]:
                dz_copy(q).wait_recv()
            else:
                e_own.wait()
        for j in range(1, ny):
            dy_copy(j, g).start()
        dc_copy(0, g).start()

    def over_core(g):
        for j in range(1, ny):
            dy_copy(j, g).wait_recv()
            dc_copy(j, g).start()

    def s_copy(q):
        return send(ss.at[q], sr.at[q], s_s.at[q], s_r.at[q], z_dev((z + nz - hops[q]) % nz))

    def shrink(g, picked):
        for j in range(ny):
            dc_copy(j, g).wait_recv()
        acc = jnp.zeros((2 * half, qg * RANK), F32)
        for e in range(nr):
            block_d = dg[e, g * qg:(g + 1) * qg].reshape(qg * RANK, fe)
            acc = acc + dot_t(picked[2 * half * g:2 * half * (g + 1), e * fe:(e + 1) * fe], block_d)
        for a in range(qg):
            first = acc[a * SLOTS:(a + 1) * SLOTS, a * RANK:(a + 1) * RANK]
            second = acc[half + a * SLOTS:half + (a + 1) * SLOTS, a * RANK:(a + 1) * RANK]
            q = g * qg + a
            if hops[q]:
                ss[q] = jnp.concatenate([first, second], axis=1)
                s_copy(q).start()
            else:
                sr[q] = jnp.concatenate([first, second], axis=1)

    def k_copy(q):
        return send(ks.at[to_z(q)], kr.at[q], k_s.at[q], k_r.at[q], z_dev(to_z(q)))

    for g in range(2, ng):
        over_z(g)
        over_y(g - 2)

    for k in range(1, nx):
        xx_copy(k).wait_recv()
    for k in range(1, nx):
        wv_copy(k).start()
        up_copy(k).start()
    for k in range(1, nx):
        wk_copy(k).wait_recv()
        wkc_copy(k).start()
    zb = nz // 2
    wide = jnp.concatenate(
        [xg[:, 2 * b:2 * b + 2].reshape(block, 128) for b in range(zb)], axis=1
    )
    turned = dot(perm, wide).astype(BF16)
    tall = 8 * nx
    for b in range(zb):
        for lb in range(lbs):
            xm[b * tall:(b + 1) * tall, lb * 128:(lb + 1) * 128] = turned[
                lb * tall:(lb + 1) * tall, b * 128:(b + 1) * 128
            ]
    picked = dot(gather, xm[...]).astype(BF16)

    for g in range(ng - 2):
        over_core(g)
    over_y(ng - 2)

    for k in range(1, nx):
        wkc_copy(k).wait_recv()
    for one in w_own:
        one.wait()
    x_rows = dot(own, xm[...]).astype(BF16)
    ks[...] = parcels(dot(x_rows, wkg[...].reshape(nx * deep, width)).astype(BF16))
    kr[nz - 1] = ks[z]
    over_y(ng - 1)
    over_core(ng - 2)
    turns(lambda q: k_copy(q).start())
    for g in range(ng - 2):
        shrink(g, picked)
    over_core(ng - 1)
    shrink(ng - 2, picked)
    shrink(ng - 1, picked)
    for k in range(1, nx):
        wv_copy(k).wait_recv()
        up_copy(k).wait_recv()
        wvc_copy(k).start()
        upc_copy(k).start()

    for q in range(nz):
        if hops[q]:
            s_copy(q).wait_recv()
    sh[x] = jnp.sum(sr[...], axis=0).astype(BF16).astype(F32)

    def sh_copy(k):
        return send(sh.at[x], sh.at[x], sh_s.at[k], sh_r.at[k], x_dev(at_x(k)))

    for k in range(1, nx):
        sh_copy(k).start()
    for k in range(1, nx):
        wvc_copy(k).wait_recv()
        upc_copy(k).wait_recv()
    vp = dot(x_rows, wvg[...].reshape(nx * deep, width))
    lane = lax.broadcasted_iota(jnp.int32, (tail, 2 * RANK), 1)
    row_l = lax.broadcasted_iota(jnp.int32, (tail, 2 * RANK), 0)
    mine = ((row_l >> 1) & 1) == (lane >= RANK).astype(jnp.int32)
    spot_o = lax.broadcasted_iota(jnp.int32, (tail, nx * SLOTS), 1) >> 3
    for k in range(1, nx):
        sh_copy(k).wait_recv()
    shrinks = sh[...].reshape(nx * SLOTS, 2 * RANK).astype(BF16)
    for xa in range(nx):
        place_a = jnp.where(spot_o == xa, place, 0.0).astype(BF16)
        low_a = jnp.where(mine, dot(place_a, shrinks), 0.0).astype(BF16)
        vp = vp + dot(low_a, jnp.concatenate([ug[xa], ug[xa]], axis=0))
    vs[...] = parcels(vp.astype(BF16))

    def v_copy(q):
        return send(vs.at[to_z(q)], vr.at[q], v_s.at[q], v_r.at[q], z_dev(to_z(q)))

    turns(lambda q: v_copy(q).start())
    vr[nz - 1] = vs[z]
    turns(lambda q: k_copy(q).wait_recv())
    ko_ref[...] = jnp.sum(kr[...].astype(F32), axis=0).astype(BF16)

    for k in range(1, nr):
        dr_copy(k).wait_send()
    for k in range(1, nx):
        for one in (wk_copy, wv_copy, up_copy, wkc_copy, wvc_copy, upc_copy):
            one(k).wait_send()
        xx_copy(k).wait_send()
        sh_copy(k).wait_send()
    for g in range(ng):
        for j in range(1, ny):
            dy_copy(j, g).wait_send()
        for j in range(ny):
            dc_copy(j, g).wait_send()

    def left(q):
        xz_copy(q).wait_send()
        k_copy(q).wait_send()

    turns(left)
    for q in range(nz):
        if hops[q]:
            s_copy(q).wait_send()
            if q >= (ng - 2) * qg:
                dz_copy(q).wait_send()

    turns(lambda q: v_copy(q).wait_recv())
    vo_ref[...] = jnp.sum(vr[...].astype(F32), axis=0).astype(BF16)
    turns(lambda q: v_copy(q).wait_send())


def shards(nr, nz, nx, hidden, adapter_ids, key_weight, value_weight, adapter_down, adapter_up):
    steps, own, wide = hidden.shape
    width = key_weight.shape[1]
    lbo = width // 128
    deep = key_weight.shape[0]
    fz = wide // nz
    lbs = fz // 128
    fe = fz // nr
    rows = nz * nx * 4
    xz = hidden.reshape(4, nz, lbs, 128).transpose(1, 0, 2, 3).reshape(nz, 4 * lbs, 128)
    dn = adapter_down.reshape(2, nr, fe, RANK).transpose(1, 0, 3, 2)
    any_, vmem = pl.BlockSpec(memory_space=pl.ANY), pl.BlockSpec(memory_space=pltpu.VMEM)
    dma = pltpu.SemaphoreType.DMA
    ng = 4 if nz >= 16 else 2
    ny = nr // CORES
    key_out, value_out = pl.pallas_call(
        functools.partial(kernel, nr, nz, nx, ng),
        out_shape=[jax.ShapeDtypeStruct((4 * lbo, 128), BF16)] * 2,
        in_specs=[any_, vmem, any_, any_, any_, any_],
        out_specs=[vmem, vmem],
        scratch_shapes=[
            pltpu.VMEM((nx, nz, 4 * lbs, 128), BF16),
            pltpu.VMEM((nx, deep, width), BF16),
            pltpu.VMEM((nx, deep, width), BF16),
            pltpu.VMEM((nx, RANK, width), BF16),
            pltpu.VMEM((nz, RANK, fe), BF16),
            pltpu.VMEM((nr, nz, RANK, fe), BF16),
            pltpu.VMEM((rows, fz), BF16),
            pltpu.VMEM((nz, SLOTS, 2 * RANK), F32),
            pltpu.VMEM((nz, SLOTS, 2 * RANK), F32),
            pltpu.VMEM((nx, SLOTS, 2 * RANK), F32),
            pltpu.VMEM((nz, 4 * lbo, 128), BF16),
            pltpu.VMEM((nz, 4 * lbo, 128), BF16),
            pltpu.VMEM((nz, 4 * lbo, 128), BF16),
            pltpu.VMEM((nz, 4 * lbo, 128), BF16),
            dma((6,)),
            dma((nz,)), dma((nz,)), dma((nx,)), dma((nx,)),
            dma((nx,)), dma((nx,)), dma((nx,)), dma((nx,)), dma((nx,)), dma((nx,)),
            dma((nx,)), dma((nx,)), dma((nx,)), dma((nx,)), dma((nx,)), dma((nx,)),
            dma((nr,)), dma((nr,)), dma((nz,)), dma((nz,)),
            dma((ny, ng)), dma((ny, ng)), dma((ny, ng)), dma((ny, ng)),
            dma((nz,)), dma((nz,)), dma((nx,)), dma((nx,)),
            dma((nz,)), dma((nz,)), dma((nz,)), dma((nz,)),
        ],
        compiler_params=pltpu.CompilerParams(
            collective_id=0, has_side_effects=True, vmem_limit_bytes=32 * 1024 * 1024
        ),
        cost_estimate=pl.CostEstimate(flops=2_000_000_000, bytes_accessed=4_000_000, transcendentals=0),
    )(xz, adapter_ids.reshape(1, rows // 2), key_weight, value_weight, dn, adapter_up[0])
    return key_out.reshape(steps, own, -1), value_out.reshape(steps, own, -1)


def solution(mesh):
    nr, tp = mesh.shape["rows"], mesh.shape["tp"]
    nx = 4 if tp >= 64 else 2
    placed = (
        P(None, ("rows", "tp"), None),
        P("rows", None),
        P("tp", None),
        P("tp", None),
        P("rows", "tp"),
        P("tp", None, None),
    )
    return jax.shard_map(
        functools.partial(shards, nr, tp // nx, nx),
        mesh=mesh,
        in_specs=placed,
        out_specs=(P(None, ("rows", "tp"), None), P(None, ("rows", "tp"), None)),
        check_vma=False,
    )
```

```python
import functools

import jax
import jax.numpy as jnp
from jax import lax
from jax.experimental import pallas as pl
from jax.experimental.pallas import tpu as pltpu
from jax.sharding import PartitionSpec as P

MESH = pl.DeviceIdType.MESH
BF16 = jnp.bfloat16
F32 = jnp.float32
CORES = 2
SLOTS = 8
RANK = 64


def dot(a, b):
    return jnp.dot(a, b, preferred_element_type=F32)


def dot_t(a, b):
    return lax.dot_general(a, b, (((1,), (1,)), ((), ())), preferred_element_type=F32)


def log2(n):
    return n.bit_length() - 1


TURNS = {16: (0, 1, 15, 2, 8, 7, 9, 6, 10, 5, 11, 4, 12, 3, 13, 14), 4: (2, 0, 1, 3)}


def kernel(
    nr, nz, nx, ng,
    x_ref, id_ref, wk_ref, wv_ref, dn_ref, up_ref,
    ko_ref, vo_ref,
    xg, wkg, wvg, ug, dsp, dg, xm, ss, sr, sh, ks, kr, vs, vr,
    loc, xz_s, xz_r, xx_s, xx_r, wk_s, wk_r, wv_s, wv_r, wkc_s, wkc_r, wvc_s, wvc_r, up_s, up_r, upc_s, upc_r,
    dr_s, dr_r, dz_s, dz_r, dy_s, dy_r, dc_s, dc_r,
    s_s, s_r, sh_s, sh_r, k_s, k_r, v_s, v_r,
):
    ny = nr // CORES
    qg = nz // ng
    lbs = x_ref.shape[1] // 4
    width = wkg.shape[2]
    lbo = width // 128
    fe = dn_ref.shape[3]
    rows = nz * nx * 4
    i = lax.axis_index("rows")
    p = lax.axis_index("tp")
    y, c = i // CORES, i % CORES
    z, x = p // nx, p % nx
    far = nz // 2

    def step(q):
        return far + (1 - 2 * (q % 2)) * ((q + 1) // 2)

    def to_z(q):
        return (z + step(q)) % nz

    hops = TURNS[nz]

    def at_x(k):
        return (x + k) % nx

    def z_dev(zz):
        return (i, zz * nx + x)

    def x_dev(xx):
        return (i, z * nx + xx)

    def r_dev(ii):
        return (ii, p)

    other = r_dev(y * CORES + 1 - c)

    def send(src, dst, ss_, rs_, dev):
        return pltpu.make_async_remote_copy(
            src_ref=src, dst_ref=dst, send_sem=ss_, recv_sem=rs_, device_id=dev, device_id_type=MESH
        )

    def turns(body):
        def one(q, t):
            body(q)
            return t

        lax.fori_loop(0, nz - 1, one, 0)

    barrier = pltpu.get_barrier_semaphore()
    turns(lambda q: pl.semaphore_signal(barrier, inc=1, device_id=z_dev(to_z(q)), device_id_type=MESH))
    for k in range(1, nr):
        pl.semaphore_signal(barrier, inc=1, device_id=r_dev((i + k) % nr), device_id_type=MESH)
    for k in range(1, nx):
        pl.semaphore_signal(barrier, inc=1, device_id=x_dev(at_x(k)), device_id_type=MESH)

    x_own = pltpu.make_async_copy(x_ref.at[z], xg.at[x, z], loc.at[0])
    d_own = pltpu.make_async_copy(dn_ref.at[i], dsp.at[pl.ds(2 * i, 2)], loc.at[1])
    w_own = (
        pltpu.make_async_copy(wk_ref, wkg.at[x], loc.at[2]),
        pltpu.make_async_copy(wv_ref, wvg.at[x], loc.at[3]),
        pltpu.make_async_copy(up_ref, ug.at[x], loc.at[4]),
    )
    for one in (x_own, d_own) + w_own:
        one.start()

    pl.semaphore_wait(barrier, nr + nx + nz - 3)

    def xz_copy(q):
        return send(x_ref.at[to_z(q)], xg.at[x, z], xz_s.at[q], xz_r.at[q], z_dev(to_z(q)))

    def dr_copy(k):
        to = (i + k) % nr
        return send(dn_ref.at[to], dsp.at[pl.ds(2 * i, 2)], dr_s.at[k], dr_r.at[k], r_dev(to))

    for k in range(1, nr):
        dr_copy(k).start()
    turns(lambda q: xz_copy(q).start())

    deep = wk_ref.shape[0]

    def share(n):
        return pl.ds(pl.multiple_of(c * (n // CORES), n // CORES), n // CORES)

    def wk_copy(k, h):
        few = deep // (2 * CORES)
        some = pl.ds(pl.multiple_of(c * (deep // CORES) + h * few, few), few)
        return send(wk_ref.at[some], wkg.at[x, some], wk_s.at[k, h], wk_r.at[k, h], x_dev(at_x(k)))

    def wv_copy(k):
        some = share(deep)
        return send(wv_ref.at[some], wvg.at[x, some], wv_s.at[k], wv_r.at[k], x_dev(at_x(k)))

    def up_copy(k):
        some = share(RANK)
        return send(up_ref.at[some], ug.at[x, some], up_s.at[k], up_r.at[k], x_dev(at_x(k)))

    def pass_on(ref, n, s_sem, r_sem, k):
        xx, some = (x + nx - k) % nx, share(n)
        return send(ref.at[xx, some], ref.at[xx, some], s_sem.at[k], r_sem.at[k], other)

    def wkc_copy(k):
        return pass_on(wkg, deep, wkc_s, wkc_r, k)

    def wvc_copy(k):
        return pass_on(wvg, deep, wvc_s, wvc_r, k)

    def upc_copy(k):
        return pass_on(ug, RANK, upc_s, upc_r, k)

    for k in range(1, nx):
        wk_copy(k, 0).start()
        up_copy(k).start()

    group = rows // 2
    ids = jnp.broadcast_to(id_ref[...].astype(F32).astype(BF16), (8, group))
    r_a = lax.broadcasted_iota(jnp.int32, (group, rows), 0)
    n_a = lax.broadcasted_iota(jnp.int32, (group, rows), 1)
    idr = dot(ids, (r_a == (n_a >> 2) * 2 + (n_a & 1)).astype(F32).astype(BF16))[:1].astype(jnp.int32)
    r_b = lax.broadcasted_iota(jnp.int32, (rows, group), 1)
    n_b = lax.broadcasted_iota(jnp.int32, (rows, group), 0)
    idc = dot_t((r_b == (n_b >> 2) * 2 + (n_b & 1)).astype(F32).astype(BF16), ids)[:, :1].astype(jnp.int32)

    bits_x, bits_lb = log2(nx), log2(lbs)
    rho_r = lax.broadcasted_iota(jnp.int32, (rows, rows), 1)
    rho_c = lax.broadcasted_iota(jnp.int32, (rows, rows), 0)
    same = (idr == idc) & (((rho_r ^ rho_c) & 2) == 0)
    slot_r = jnp.sum((same & (rho_c < rho_r)).astype(F32), axis=0, keepdims=True).astype(jnp.int32)
    slot_c = jnp.sum((same & (rho_r < rho_c)).astype(F32), axis=1, keepdims=True).astype(jnp.int32)
    half = qg * SLOTS
    slots = 2 * nz * SLOTS
    sig = lax.broadcasted_iota(jnp.int32, (slots, rows), 0)
    rho = lax.broadcasted_iota(jnp.int32, (slots, rows), 1)
    t_sig = (sig >> log2(half)) & 1
    col_sig = lax.broadcasted_iota(jnp.int32, (slots, 1), 0)
    q_sig = (col_sig >> log2(2 * half)) * qg + ((col_sig & (half - 1)) >> 3)
    za_sig = jnp.zeros((slots, 1), jnp.int32)
    for q in range(nz):
        za_sig = jnp.where(q_sig == q, (z + nz - hops[q]) % nz, za_sig)
    gather = (
        (idr == za_sig * nx + x) & (slot_r == (sig & (SLOTS - 1))) & (((rho >> 1) & 1) == t_sig)
    ).astype(F32).astype(BF16)
    spot = lax.broadcasted_iota(jnp.int32, (rows, nx * SLOTS), 1)
    place = (
        (idc == z * nx + (spot >> 3)) & (slot_c == (spot & (SLOTS - 1)))
    ).astype(F32).astype(BF16)

    block = 2 * nx * 4 * lbs
    o = lax.broadcasted_iota(jnp.int32, (block, block), 0)
    n = lax.broadcasted_iota(jnp.int32, (block, block), 1)
    r_o = o & 3
    x_o = (o >> 2) & (nx - 1)
    z_o = (o >> (2 + bits_x)) & 1
    l_o = o >> (3 + bits_x)
    perm = (n == ((((x_o * 2 + z_o) * 4 + r_o) << bits_lb) + l_o)).astype(F32).astype(BF16)

    tail = nz * 4
    o_own = lax.broadcasted_iota(jnp.int32, (tail, rows), 0)
    n_own = lax.broadcasted_iota(jnp.int32, (tail, rows), 1)
    own = (n_own == (o_own >> 2) * (4 * nx) + 4 * x + (o_own & 3)).astype(F32).astype(BF16)
    place = dot(own, place)
    big = tail * lbo
    o_out = lax.broadcasted_iota(jnp.int32, (big, big), 0)
    n_out = lax.broadcasted_iota(jnp.int32, (big, big), 1)
    spread = (
        n_out == (o_out & (lbo - 1)) * tail + (o_out >> log2(lbo))
    ).astype(F32).astype(BF16)

    def parcels(part):
        tall = jnp.concatenate([part[:, lb * 128:(lb + 1) * 128] for lb in range(lbo)], axis=0)
        return dot(spread, tall).astype(BF16).reshape(nz, 4 * lbo, 128)

    for k in range(1, nr):
        dr_copy(k).wait_recv()
    d_own.wait()

    def dz_copy(q):
        to = (z + hops[q]) % nz
        return send(dsp.at[to], dg.at[i, q], dz_s.at[q], dz_r.at[q], z_dev(to))

    def over_z(g):
        if g > 1:
            for q in range((g - 2) * qg, (g - 1) * qg):
                if hops[q]:
                    dz_copy(q).wait_send()
        for q in range(g * qg, (g + 1) * qg):
            if hops[q]:
                dz_copy(q).start()

    over_z(0)
    over_z(1)
    e_own = pltpu.make_async_copy(dsp.at[z], dg.at[i, hops.index(0)], loc.at[5])
    e_own.start()

    turns(lambda q: xz_copy(q).wait_recv())
    x_own.wait()

    def xx_copy(k):
        return send(xg.at[x], xg.at[x], xx_s.at[k], xx_r.at[k], x_dev(at_x(k)))

    for k in range(1, nx):
        xx_copy(k).start()

    def dy_copy(j, g):
        some = pl.ds(g * qg, qg)
        to = ((y + j) % ny) * CORES + c
        return send(dg.at[i, some], dg.at[i, some], dy_s.at[j, g], dy_r.at[j, g], r_dev(to))

    def dc_copy(j, g):
        some = pl.ds(g * qg, qg)
        e = ((y + ny - j) % ny) * CORES + c
        return send(dg.at[e, some], dg.at[e, some], dc_s.at[j, g], dc_r.at[j, g], other)

    def over_y(g):
        for q in range(g * qg, (g + 1) * qg):
            if hops[q]:
                dz_copy(q).wait_recv()
            else:
                e_own.wait()
        for j in range(1, ny):
            dy_copy(j, g).start()
        dc_copy(0, g).start()

    def over_core(g):
        for j in range(1, ny):
            dy_copy(j, g).wait_recv()
            dc_copy(j, g).start()

    def s_copy(q):
        return send(ss.at[q], sr.at[q], s_s.at[q], s_r.at[q], z_dev((z + nz - hops[q]) % nz))

    def shrink(g, picked):
        for j in range(ny):
            dc_copy(j, g).wait_recv()
        acc = jnp.zeros((2 * half, qg * RANK), F32)
        for e in range(nr):
            block_d = dg[e, g * qg:(g + 1) * qg].reshape(qg * RANK, fe)
            acc = acc + dot_t(picked[2 * half * g:2 * half * (g + 1), e * fe:(e + 1) * fe], block_d)
        for a in range(qg):
            first = acc[a * SLOTS:(a + 1) * SLOTS, a * RANK:(a + 1) * RANK]
            second = acc[half + a * SLOTS:half + (a + 1) * SLOTS, a * RANK:(a + 1) * RANK]
            q = g * qg + a
            if hops[q]:
                ss[q] = jnp.concatenate([first, second], axis=1)
                s_copy(q).start()
            else:
                sr[q] = jnp.concatenate([first, second], axis=1)

    def k_copy(q):
        return send(ks.at[to_z(q)], kr.at[q], k_s.at[q], k_r.at[q], z_dev(to_z(q)))

    for g in range(2, ng):
        over_z(g)
    over_y(0)

    for k in range(1, nx):
        xx_copy(k).wait_recv()
    for k in range(1, nx):
        wk_copy(k, 1).start()
    for k in range(1, nx):
        wv_copy(k).start()
    zb = nz // 2
    wide = jnp.concatenate(
        [xg[:, 2 * b:2 * b + 2].reshape(block, 128) for b in range(zb)], axis=1
    )
    turned = dot(perm, wide).astype(BF16)
    tall = 8 * nx
    for b in range(zb):
        for lb in range(lbs):
            xm[b * tall:(b + 1) * tall, lb * 128:(lb + 1) * 128] = turned[
                lb * tall:(lb + 1) * tall, b * 128:(b + 1) * 128
            ]
    picked = dot(gather, xm[...]).astype(BF16)

    for g in range(1, ng):
        over_y(g)
        over_core(g - 1)
    for g in range(ng - 2):
        shrink(g, picked)
    over_core(ng - 1)
    shrink(ng - 2, picked)
    shrink(ng - 1, picked)

    for k in range(1, nx):
        for h in range(2):
            wk_copy(k, h).wait_recv()
        wkc_copy(k).start()
    x_rows = dot(own, xm[...]).astype(BF16)
    for one in w_own:
        one.wait()
    for k in range(1, nx):
        wkc_copy(k).wait_recv()
    ks[...] = parcels(dot(x_rows, wkg[...].reshape(nx * deep, width)).astype(BF16))
    turns(lambda q: k_copy(q).start())
    kr[nz - 1] = ks[z]

    for k in range(1, nx):
        up_copy(k).wait_recv()
        upc_copy(k).start()
    for q in range(nz):
        if hops[q]:
            s_copy(q).wait_recv()
    sh[x] = jnp.sum(sr[...], axis=0).astype(BF16).astype(F32)

    def sh_copy(k):
        return send(sh.at[x], sh.at[x], sh_s.at[k], sh_r.at[k], x_dev(at_x(k)))

    for k in range(1, nx):
        sh_copy(k).start()
    for k in range(1, nx):
        wv_copy(k).wait_recv()
        wvc_copy(k).start()
    for k in range(1, nx):
        wvc_copy(k).wait_recv()
        upc_copy(k).wait_recv()
    vp = dot(x_rows, wvg[...].reshape(nx * deep, width))
    lane = lax.broadcasted_iota(jnp.int32, (tail, 2 * RANK), 1)
    row_l = lax.broadcasted_iota(jnp.int32, (tail, 2 * RANK), 0)
    mine = ((row_l >> 1) & 1) == (lane >= RANK).astype(jnp.int32)
    spot_o = lax.broadcasted_iota(jnp.int32, (tail, nx * SLOTS), 1) >> 3
    for k in range(1, nx):
        sh_copy(k).wait_recv()
    shrinks = sh[...].reshape(nx * SLOTS, 2 * RANK).astype(BF16)
    for xa in range(nx):
        place_a = jnp.where(spot_o == xa, place, 0.0).astype(BF16)
        low_a = jnp.where(mine, dot(place_a, shrinks), 0.0).astype(BF16)
        vp = vp + dot(low_a, jnp.concatenate([ug[xa], ug[xa]], axis=0))
    vs[...] = parcels(vp.astype(BF16))

    def v_copy(q):
        return send(vs.at[to_z(q)], vr.at[q], v_s.at[q], v_r.at[q], z_dev(to_z(q)))

    turns(lambda q: v_copy(q).start())
    vr[nz - 1] = vs[z]
    turns(lambda q: k_copy(q).wait_recv())
    ko_ref[...] = jnp.sum(kr[...].astype(F32), axis=0).astype(BF16)

    for k in range(1, nr):
        dr_copy(k).wait_send()
    for k in range(1, nx):
        for h in range(2):
            wk_copy(k, h).wait_send()
        for one in (wv_copy, up_copy, wkc_copy, wvc_copy, upc_copy):
            one(k).wait_send()
        xx_copy(k).wait_send()
        sh_copy(k).wait_send()
    for g in range(ng):
        for j in range(1, ny):
            dy_copy(j, g).wait_send()
        for j in range(ny):
            dc_copy(j, g).wait_send()

    def left(q):
        xz_copy(q).wait_send()
        k_copy(q).wait_send()

    turns(left)
    for q in range(nz):
        if hops[q]:
            s_copy(q).wait_send()
            if q >= (ng - 2) * qg:
                dz_copy(q).wait_send()

    turns(lambda q: v_copy(q).wait_recv())
    vo_ref[...] = jnp.sum(vr[...].astype(F32), axis=0).astype(BF16)
    turns(lambda q: v_copy(q).wait_send())


def shards(nr, nz, nx, hidden, adapter_ids, key_weight, value_weight, adapter_down, adapter_up):
    steps, own, wide = hidden.shape
    width = key_weight.shape[1]
    lbo = width // 128
    deep = key_weight.shape[0]
    fz = wide // nz
    lbs = fz // 128
    fe = fz // nr
    rows = nz * nx * 4
    xz = hidden.reshape(4, nz, lbs, 128).transpose(1, 0, 2, 3).reshape(nz, 4 * lbs, 128)
    dn = adapter_down.reshape(2, nr, fe, RANK).transpose(1, 0, 3, 2)
    any_, vmem = pl.BlockSpec(memory_space=pl.ANY), pl.BlockSpec(memory_space=pltpu.VMEM)
    dma = pltpu.SemaphoreType.DMA
    ng = 4 if nz >= 16 else 2
    ny = nr // CORES
    key_out, value_out = pl.pallas_call(
        functools.partial(kernel, nr, nz, nx, ng),
        out_shape=[jax.ShapeDtypeStruct((4 * lbo, 128), BF16)] * 2,
        in_specs=[any_, vmem, any_, any_, any_, any_],
        out_specs=[vmem, vmem],
        scratch_shapes=[
            pltpu.VMEM((nx, nz, 4 * lbs, 128), BF16),
            pltpu.VMEM((nx, deep, width), BF16),
            pltpu.VMEM((nx, deep, width), BF16),
            pltpu.VMEM((nx, RANK, width), BF16),
            pltpu.VMEM((nz, RANK, fe), BF16),
            pltpu.VMEM((nr, nz, RANK, fe), BF16),
            pltpu.VMEM((rows, fz), BF16),
            pltpu.VMEM((nz, SLOTS, 2 * RANK), F32),
            pltpu.VMEM((nz, SLOTS, 2 * RANK), F32),
            pltpu.VMEM((nx, SLOTS, 2 * RANK), F32),
            pltpu.VMEM((nz, 4 * lbo, 128), BF16),
            pltpu.VMEM((nz, 4 * lbo, 128), BF16),
            pltpu.VMEM((nz, 4 * lbo, 128), BF16),
            pltpu.VMEM((nz, 4 * lbo, 128), BF16),
            dma((6,)),
            dma((nz,)), dma((nz,)), dma((nx,)), dma((nx,)),
            dma((nx, 2)), dma((nx, 2)), dma((nx,)), dma((nx,)), dma((nx,)), dma((nx,)),
            dma((nx,)), dma((nx,)), dma((nx,)), dma((nx,)), dma((nx,)), dma((nx,)),
            dma((nr,)), dma((nr,)), dma((nz,)), dma((nz,)),
            dma((ny, ng)), dma((ny, ng)), dma((ny, ng)), dma((ny, ng)),
            dma((nz,)), dma((nz,)), dma((nx,)), dma((nx,)),
            dma((nz,)), dma((nz,)), dma((nz,)), dma((nz,)),
        ],
        compiler_params=pltpu.CompilerParams(
            collective_id=0, has_side_effects=True, vmem_limit_bytes=32 * 1024 * 1024
        ),
        cost_estimate=pl.CostEstimate(flops=2_000_000_000, bytes_accessed=4_000_000, transcendentals=0),
    )(xz, adapter_ids.reshape(1, rows // 2), key_weight, value_weight, dn, adapter_up[0])
    return key_out.reshape(steps, own, -1), value_out.reshape(steps, own, -1)


def solution(mesh):
    nr, tp = mesh.shape["rows"], mesh.shape["tp"]
    nx = 4 if tp >= 64 else 2
    placed = (
        P(None, ("rows", "tp"), None),
        P("rows", None),
        P("tp", None),
        P("tp", None),
        P("rows", "tp"),
        P("tp", None, None),
    )
    return jax.shard_map(
        functools.partial(shards, nr, tp // nx, nx),
        mesh=mesh,
        in_specs=placed,
        out_specs=(P(None, ("rows", "tp"), None), P(None, ("rows", "tp"), None)),
        check_vma=False,
    )
```

```python
import functools

import jax
import jax.numpy as jnp
from jax import lax
from jax.experimental import pallas as pl
from jax.experimental.pallas import tpu as pltpu
from jax.sharding import PartitionSpec as P

MESH = pl.DeviceIdType.MESH
BF16 = jnp.bfloat16
F32 = jnp.float32
CORES = 2
SLOTS = 8
RANK = 64


def dot(a, b):
    return jnp.dot(a, b, preferred_element_type=F32)


def dot_t(a, b):
    return lax.dot_general(a, b, (((1,), (1,)), ((), ())), preferred_element_type=F32)


def log2(n):
    return n.bit_length() - 1


TURNS = {16: (0, 1, 15, 2, 8, 7, 9, 6, 10, 5, 11, 4, 12, 3, 13, 14), 4: (2, 0, 1, 3)}


def kernel(
    nr, nz, nx, ng,
    x_ref, id_ref, wk_ref, wv_ref, dn_ref, up_ref,
    ko_ref, vo_ref,
    xg, wkg, wvg, ug, dsp, dg, xm, ss, sr, sh, ks, kr, vs, vr,
    loc, xz_s, xz_r, xx_s, xx_r, wk_s, wk_r, wv_s, wv_r, wkc_s, wkc_r, wvc_s, wvc_r, up_s, up_r, upc_s, upc_r,
    dr_s, dr_r, dz_s, dz_r, dy_s, dy_r, dc_s, dc_r,
    s_s, s_r, sh_s, sh_r, k_s, k_r, v_s, v_r,
):
    ny = nr // CORES
    qg = nz // ng
    lbs = x_ref.shape[1] // 4
    width = wkg.shape[2]
    lbo = width // 128
    fe = dn_ref.shape[3]
    rows = nz * nx * 4
    i = lax.axis_index("rows")
    p = lax.axis_index("tp")
    y, c = i // CORES, i % CORES
    z, x = p // nx, p % nx
    far = nz // 2

    def step(q):
        return far + (1 - 2 * (q % 2)) * ((q + 1) // 2)

    def to_z(q):
        return (z + step(q)) % nz

    hops = TURNS[nz]

    def at_x(k):
        return (x + k) % nx

    def z_dev(zz):
        return (i, zz * nx + x)

    def x_dev(xx):
        return (i, z * nx + xx)

    def r_dev(ii):
        return (ii, p)

    other = r_dev(y * CORES + 1 - c)

    def send(src, dst, ss_, rs_, dev):
        return pltpu.make_async_remote_copy(
            src_ref=src, dst_ref=dst, send_sem=ss_, recv_sem=rs_, device_id=dev, device_id_type=MESH
        )

    def turns(body):
        def one(q, t):
            body(q)
            return t

        lax.fori_loop(0, nz - 1, one, 0)

    barrier = pltpu.get_barrier_semaphore()
    turns(lambda q: pl.semaphore_signal(barrier, inc=1, device_id=z_dev(to_z(q)), device_id_type=MESH))
    for k in range(1, nr):
        pl.semaphore_signal(barrier, inc=1, device_id=r_dev((i + k) % nr), device_id_type=MESH)
    for k in range(1, nx):
        pl.semaphore_signal(barrier, inc=1, device_id=x_dev(at_x(k)), device_id_type=MESH)

    x_own = pltpu.make_async_copy(x_ref.at[z], xg.at[x, z], loc.at[0])
    d_own = pltpu.make_async_copy(dn_ref.at[i], dsp.at[pl.ds(2 * i, 2)], loc.at[1])
    w_own = (
        pltpu.make_async_copy(wk_ref, wkg.at[x], loc.at[2]),
        pltpu.make_async_copy(wv_ref, wvg.at[x], loc.at[3]),
        pltpu.make_async_copy(up_ref, ug.at[x], loc.at[4]),
    )
    for one in (x_own, d_own) + w_own:
        one.start()

    pl.semaphore_wait(barrier, nr + nx + nz - 3)

    def xz_copy(q):
        return send(x_ref.at[to_z(q)], xg.at[x, z], xz_s.at[q], xz_r.at[q], z_dev(to_z(q)))

    def dr_copy(k):
        to = (i + k) % nr
        return send(dn_ref.at[to], dsp.at[pl.ds(2 * i, 2)], dr_s.at[k], dr_r.at[k], r_dev(to))

    for k in range(1, nr):
        dr_copy(k).start()
    turns(lambda q: xz_copy(q).start())

    deep = wk_ref.shape[0]

    def share(n):
        return pl.ds(pl.multiple_of(c * (n // CORES), n // CORES), n // CORES)

    def wk_copy(k, h):
        few = deep // (2 * CORES)
        some = pl.ds(pl.multiple_of(c * (deep // CORES) + h * few, few), few)
        return send(wk_ref.at[some], wkg.at[x, some], wk_s.at[k, h], wk_r.at[k, h], x_dev(at_x(k)))

    def wv_copy(k):
        some = share(deep)
        return send(wv_ref.at[some], wvg.at[x, some], wv_s.at[k], wv_r.at[k], x_dev(at_x(k)))

    def up_copy(k):
        some = share(RANK)
        return send(up_ref.at[some], ug.at[x, some], up_s.at[k], up_r.at[k], x_dev(at_x(k)))

    def pass_on(ref, n, s_sem, r_sem, k):
        xx, some = (x + nx - k) % nx, share(n)
        return send(ref.at[xx, some], ref.at[xx, some], s_sem.at[k], r_sem.at[k], other)

    def wkc_copy(k):
        return pass_on(wkg, deep, wkc_s, wkc_r, k)

    def wvc_copy(k):
        return pass_on(wvg, deep, wvc_s, wvc_r, k)

    def upc_copy(k):
        return pass_on(ug, RANK, upc_s, upc_r, k)

    for k in range(1, nx):
        wk_copy(k, 0).start()
        up_copy(k).start()

    group = rows // 2
    ids = jnp.broadcast_to(id_ref[...].astype(F32).astype(BF16), (8, group))
    r_a = lax.broadcasted_iota(jnp.int32, (group, rows), 0)
    n_a = lax.broadcasted_iota(jnp.int32, (group, rows), 1)
    idr = dot(ids, (r_a == (n_a >> 2) * 2 + (n_a & 1)).astype(F32).astype(BF16))[:1].astype(jnp.int32)
    r_b = lax.broadcasted_iota(jnp.int32, (rows, group), 1)
    n_b = lax.broadcasted_iota(jnp.int32, (rows, group), 0)
    idc = dot_t((r_b == (n_b >> 2) * 2 + (n_b & 1)).astype(F32).astype(BF16), ids)[:, :1].astype(jnp.int32)

    bits_x, bits_lb = log2(nx), log2(lbs)
    rho_r = lax.broadcasted_iota(jnp.int32, (rows, rows), 1)
    rho_c = lax.broadcasted_iota(jnp.int32, (rows, rows), 0)
    same = (idr == idc) & (((rho_r ^ rho_c) & 2) == 0)
    slot_r = jnp.sum((same & (rho_c < rho_r)).astype(F32), axis=0, keepdims=True).astype(jnp.int32)
    slot_c = jnp.sum((same & (rho_r < rho_c)).astype(F32), axis=1, keepdims=True).astype(jnp.int32)
    half = qg * SLOTS
    slots = 2 * nz * SLOTS
    sig = lax.broadcasted_iota(jnp.int32, (slots, rows), 0)
    rho = lax.broadcasted_iota(jnp.int32, (slots, rows), 1)
    t_sig = (sig >> log2(half)) & 1
    col_sig = lax.broadcasted_iota(jnp.int32, (slots, 1), 0)
    q_sig = (col_sig >> log2(2 * half)) * qg + ((col_sig & (half - 1)) >> 3)
    za_sig = jnp.zeros((slots, 1), jnp.int32)
    for q in range(nz):
        za_sig = jnp.where(q_sig == q, (z + nz - hops[q]) % nz, za_sig)
    gather = (
        (idr == za_sig * nx + x) & (slot_r == (sig & (SLOTS - 1))) & (((rho >> 1) & 1) == t_sig)
    ).astype(F32).astype(BF16)
    spot = lax.broadcasted_iota(jnp.int32, (rows, nx * SLOTS), 1)
    place = (
        (idc == z * nx + (spot >> 3)) & (slot_c == (spot & (SLOTS - 1)))
    ).astype(F32).astype(BF16)

    block = 2 * nx * 4 * lbs
    o = lax.broadcasted_iota(jnp.int32, (block, block), 0)
    n = lax.broadcasted_iota(jnp.int32, (block, block), 1)
    r_o = o & 3
    x_o = (o >> 2) & (nx - 1)
    z_o = (o >> (2 + bits_x)) & 1
    l_o = o >> (3 + bits_x)
    perm = (n == ((((x_o * 2 + z_o) * 4 + r_o) << bits_lb) + l_o)).astype(F32).astype(BF16)

    tail = nz * 4
    o_own = lax.broadcasted_iota(jnp.int32, (tail, rows), 0)
    n_own = lax.broadcasted_iota(jnp.int32, (tail, rows), 1)
    own = (n_own == (o_own >> 2) * (4 * nx) + 4 * x + (o_own & 3)).astype(F32).astype(BF16)
    place = dot(own, place)
    big = tail * lbo
    o_out = lax.broadcasted_iota(jnp.int32, (big, big), 0)
    n_out = lax.broadcasted_iota(jnp.int32, (big, big), 1)
    spread = (
        n_out == (o_out & (lbo - 1)) * tail + (o_out >> log2(lbo))
    ).astype(F32).astype(BF16)

    def parcels(part):
        tall = jnp.concatenate([part[:, lb * 128:(lb + 1) * 128] for lb in range(lbo)], axis=0)
        return dot(spread, tall).astype(BF16).reshape(nz, 4 * lbo, 128)

    for k in range(1, nr):
        dr_copy(k).wait_recv()
    d_own.wait()

    def dz_copy(q):
        to = (z + hops[q]) % nz
        return send(dsp.at[to], dg.at[i, q], dz_s.at[q], dz_r.at[q], z_dev(to))

    def over_z(g):
        if g > 1:
            for q in range((g - 2) * qg, (g - 1) * qg):
                if hops[q]:
                    dz_copy(q).wait_send()
        for q in range(g * qg, (g + 1) * qg):
            if hops[q]:
                dz_copy(q).start()

    over_z(0)
    over_z(1)
    e_own = pltpu.make_async_copy(dsp.at[z], dg.at[i, hops.index(0)], loc.at[5])
    e_own.start()

    turns(lambda q: xz_copy(q).wait_recv())
    x_own.wait()

    def xx_copy(k):
        return send(xg.at[x], xg.at[x], xx_s.at[k], xx_r.at[k], x_dev(at_x(k)))

    for k in range(1, nx):
        xx_copy(k).start()

    def dy_copy(j, g):
        some = pl.ds(g * qg, qg)
        to = ((y + j) % ny) * CORES + c
        return send(dg.at[i, some], dg.at[i, some], dy_s.at[j, g], dy_r.at[j, g], r_dev(to))

    def dc_copy(j, g):
        some = pl.ds(g * qg, qg)
        e = ((y + ny - j) % ny) * CORES + c
        return send(dg.at[e, some], dg.at[e, some], dc_s.at[j, g], dc_r.at[j, g], other)

    def over_y(g):
        for q in range(g * qg, (g + 1) * qg):
            if hops[q]:
                dz_copy(q).wait_recv()
            else:
                e_own.wait()
        for j in range(1, ny):
            dy_copy(j, g).start()
        dc_copy(0, g).start()

    def over_core(g):
        for j in range(1, ny):
            dy_copy(j, g).wait_recv()
            dc_copy(j, g).start()

    def s_copy(q):
        return send(ss.at[q], sr.at[q], s_s.at[q], s_r.at[q], z_dev((z + nz - hops[q]) % nz))

    def shrink(g, picked):
        for j in range(ny):
            dc_copy(j, g).wait_recv()
        acc = jnp.zeros((2 * half, qg * RANK), F32)
        for e in range(0, nr, 2):
            block_d = jnp.concatenate(
                [dg[e + b, g * qg:(g + 1) * qg].reshape(qg * RANK, fe) for b in range(2)], axis=1
            )
            acc = acc + dot_t(picked[2 * half * g:2 * half * (g + 1), e * fe:(e + 2) * fe], block_d)
        for a in range(qg):
            first = acc[a * SLOTS:(a + 1) * SLOTS, a * RANK:(a + 1) * RANK]
            second = acc[half + a * SLOTS:half + (a + 1) * SLOTS, a * RANK:(a + 1) * RANK]
            q = g * qg + a
            if hops[q]:
                ss[q] = jnp.concatenate([first, second], axis=1)
                s_copy(q).start()
            else:
                sr[q] = jnp.concatenate([first, second], axis=1)

    def k_copy(q):
        return send(ks.at[to_z(q)], kr.at[q], k_s.at[q], k_r.at[q], z_dev(to_z(q)))

    for g in range(2, ng):
        over_z(g)
    over_y(0)

    for k in range(1, nx):
        xx_copy(k).wait_recv()
    for k in range(1, nx):
        wk_copy(k, 1).start()
    for k in range(1, nx):
        wv_copy(k).start()
    zb = nz // 2
    wide = jnp.concatenate(
        [xg[:, 2 * b:2 * b + 2].reshape(block, 128) for b in range(zb)], axis=1
    )
    turned = dot(perm, wide).astype(BF16)
    tall = 8 * nx
    for b in range(zb):
        for lb in range(lbs):
            xm[b * tall:(b + 1) * tall, lb * 128:(lb + 1) * 128] = turned[
                lb * tall:(lb + 1) * tall, b * 128:(b + 1) * 128
            ]
    picked = dot(gather, xm[...]).astype(BF16)

    for g in range(1, ng):
        over_y(g)
        if g > 1:
            over_core(g - 2)
    over_core(ng - 2)
    for g in range(ng - 2):
        shrink(g, picked)
    over_core(ng - 1)
    shrink(ng - 2, picked)
    shrink(ng - 1, picked)

    for k in range(1, nx):
        for h in range(2):
            wk_copy(k, h).wait_recv()
        wkc_copy(k).start()
    x_rows = dot(own, xm[...]).astype(BF16)
    for one in w_own:
        one.wait()
    for k in range(1, nx):
        wkc_copy(k).wait_recv()
    ks[...] = parcels(dot(x_rows, wkg[...].reshape(nx * deep, width)).astype(BF16))
    turns(lambda q: k_copy(q).start())
    kr[nz - 1] = ks[z]

    for k in range(1, nx):
        up_copy(k).wait_recv()
        upc_copy(k).start()
    for q in range(nz):
        if hops[q]:
            s_copy(q).wait_recv()
    sh[x] = jnp.sum(sr[...], axis=0).astype(BF16).astype(F32)

    def sh_copy(k):
        return send(sh.at[x], sh.at[x], sh_s.at[k], sh_r.at[k], x_dev(at_x(k)))

    for k in range(1, nx):
        sh_copy(k).start()
    for k in range(1, nx):
        wv_copy(k).wait_recv()
        wvc_copy(k).start()
    for k in range(1, nx):
        wvc_copy(k).wait_recv()
        upc_copy(k).wait_recv()
    vp = dot(x_rows, wvg[...].reshape(nx * deep, width))
    lane = lax.broadcasted_iota(jnp.int32, (tail, 2 * RANK), 1)
    row_l = lax.broadcasted_iota(jnp.int32, (tail, 2 * RANK), 0)
    mine = ((row_l >> 1) & 1) == (lane >= RANK).astype(jnp.int32)
    spot_o = lax.broadcasted_iota(jnp.int32, (tail, nx * SLOTS), 1) >> 3
    places = [jnp.where(spot_o == xa, place, 0.0).astype(BF16) for xa in range(nx)]
    for k in range(1, nx):
        sh_copy(k).wait_recv()
    shrinks = sh[...].reshape(nx * SLOTS, 2 * RANK).astype(BF16)
    lows = []
    for xa in range(nx):
        low_a = jnp.where(mine, dot(places[xa], shrinks), 0.0)
        lows.append(low_a + jnp.concatenate([low_a[:, RANK:], low_a[:, :RANK]], axis=1))
    low = jnp.concatenate(
        [jnp.where(lane < RANK, lows[xa], lows[xa + 1]) for xa in range(0, nx, 2)], axis=1
    ).astype(BF16)
    vp = vp + dot(low, ug[...].reshape(nx * RANK, width))
    vs[...] = parcels(vp.astype(BF16))

    def v_copy(q):
        return send(vs.at[to_z(q)], vr.at[q], v_s.at[q], v_r.at[q], z_dev(to_z(q)))

    turns(lambda q: v_copy(q).start())
    vr[nz - 1] = vs[z]
    turns(lambda q: k_copy(q).wait_recv())
    ko_ref[...] = jnp.sum(kr[...].astype(F32), axis=0).astype(BF16)

    for k in range(1, nr):
        dr_copy(k).wait_send()
    for k in range(1, nx):
        for h in range(2):
            wk_copy(k, h).wait_send()
        for one in (wv_copy, up_copy, wkc_copy, wvc_copy, upc_copy):
            one(k).wait_send()
        xx_copy(k).wait_send()
        sh_copy(k).wait_send()
    for g in range(ng):
        for j in range(1, ny):
            dy_copy(j, g).wait_send()
        for j in range(ny):
            dc_copy(j, g).wait_send()

    def left(q):
        xz_copy(q).wait_send()
        k_copy(q).wait_send()

    turns(left)
    for q in range(nz):
        if hops[q]:
            s_copy(q).wait_send()
            if q >= (ng - 2) * qg:
                dz_copy(q).wait_send()

    turns(lambda q: v_copy(q).wait_recv())
    vo_ref[...] = jnp.sum(vr[...].astype(F32), axis=0).astype(BF16)
    turns(lambda q: v_copy(q).wait_send())


def shards(nr, nz, nx, hidden, adapter_ids, key_weight, value_weight, adapter_down, adapter_up):
    steps, own, wide = hidden.shape
    width = key_weight.shape[1]
    lbo = width // 128
    deep = key_weight.shape[0]
    fz = wide // nz
    lbs = fz // 128
    fe = fz // nr
    rows = nz * nx * 4
    xz = hidden.reshape(4, nz, lbs, 128).transpose(1, 0, 2, 3).reshape(nz, 4 * lbs, 128)
    dn = adapter_down.reshape(2, nr, fe, RANK).transpose(1, 0, 3, 2)
    any_, vmem = pl.BlockSpec(memory_space=pl.ANY), pl.BlockSpec(memory_space=pltpu.VMEM)
    dma = pltpu.SemaphoreType.DMA
    ng = 4 if nz >= 16 else 2
    ny = nr // CORES
    key_out, value_out = pl.pallas_call(
        functools.partial(kernel, nr, nz, nx, ng),
        out_shape=[jax.ShapeDtypeStruct((4 * lbo, 128), BF16)] * 2,
        in_specs=[any_, vmem, any_, any_, any_, any_],
        out_specs=[vmem, vmem],
        scratch_shapes=[
            pltpu.VMEM((nx, nz, 4 * lbs, 128), BF16),
            pltpu.VMEM((nx, deep, width), BF16),
            pltpu.VMEM((nx, deep, width), BF16),
            pltpu.VMEM((nx, RANK, width), BF16),
            pltpu.VMEM((nz, RANK, fe), BF16),
            pltpu.VMEM((nr, nz, RANK, fe), BF16),
            pltpu.VMEM((rows, fz), BF16),
            pltpu.VMEM((nz, SLOTS, 2 * RANK), F32),
            pltpu.VMEM((nz, SLOTS, 2 * RANK), F32),
            pltpu.VMEM((nx, SLOTS, 2 * RANK), F32),
            pltpu.VMEM((nz, 4 * lbo, 128), BF16),
            pltpu.VMEM((nz, 4 * lbo, 128), BF16),
            pltpu.VMEM((nz, 4 * lbo, 128), BF16),
            pltpu.VMEM((nz, 4 * lbo, 128), BF16),
            dma((6,)),
            dma((nz,)), dma((nz,)), dma((nx,)), dma((nx,)),
            dma((nx, 2)), dma((nx, 2)), dma((nx,)), dma((nx,)), dma((nx,)), dma((nx,)),
            dma((nx,)), dma((nx,)), dma((nx,)), dma((nx,)), dma((nx,)), dma((nx,)),
            dma((nr,)), dma((nr,)), dma((nz,)), dma((nz,)),
            dma((ny, ng)), dma((ny, ng)), dma((ny, ng)), dma((ny, ng)),
            dma((nz,)), dma((nz,)), dma((nx,)), dma((nx,)),
            dma((nz,)), dma((nz,)), dma((nz,)), dma((nz,)),
        ],
        compiler_params=pltpu.CompilerParams(
            collective_id=0, has_side_effects=True, vmem_limit_bytes=32 * 1024 * 1024
        ),
        cost_estimate=pl.CostEstimate(flops=2_000_000_000, bytes_accessed=4_000_000, transcendentals=0),
    )(xz, adapter_ids.reshape(1, rows // 2), key_weight, value_weight, dn, adapter_up[0])
    return key_out.reshape(steps, own, -1), value_out.reshape(steps, own, -1)


def solution(mesh):
    nr, tp = mesh.shape["rows"], mesh.shape["tp"]
    nx = 4 if tp >= 64 else 2
    placed = (
        P(None, ("rows", "tp"), None),
        P("rows", None),
        P("tp", None),
        P("tp", None),
        P("rows", "tp"),
        P("tp", None, None),
    )
    return jax.shard_map(
        functools.partial(shards, nr, tp // nx, nx),
        mesh=mesh,
        in_specs=placed,
        out_specs=(P(None, ("rows", "tp"), None), P(None, ("rows", "tp"), None)),
        check_vma=False,
    )
```

```python
import functools

import jax
import jax.numpy as jnp
from jax import lax
from jax.experimental import pallas as pl
from jax.experimental.pallas import tpu as pltpu
from jax.sharding import PartitionSpec as P

MESH = pl.DeviceIdType.MESH
BF16 = jnp.bfloat16
F32 = jnp.float32
CORES = 2
SLOTS = 8
RANK = 64


def dot(a, b):
    return jnp.dot(a, b, preferred_element_type=F32)


def dot_t(a, b):
    return lax.dot_general(a, b, (((1,), (1,)), ((), ())), preferred_element_type=F32)


def log2(n):
    return n.bit_length() - 1


TURNS = {16: (8, 0, 1, 15, 7, 9, 2, 14, 6, 10, 3, 13, 5, 11, 4, 12), 4: (2, 0, 1, 3)}


def kernel(
    nr, nz, nx, ng,
    x_ref, id_ref, wk_ref, wv_ref, dn_ref, up_ref,
    ko_ref, vo_ref,
    xg, wkg, wvg, ug, dsp, dg, xm, ss, sr, sh, ks, kr, vs, vr,
    loc, xz_s, xz_r, xx_s, xx_r, wk_s, wk_r, wv_s, wv_r, wkc_s, wkc_r, wvc_s, wvc_r, up_s, up_r, upc_s, upc_r,
    dr_s, dr_r, dz_s, dz_r, dy_s, dy_r, dc_s, dc_r,
    s_s, s_r, sh_s, sh_r, k_s, k_r, v_s, v_r,
):
    ny = nr // CORES
    qg = nz // ng
    lbs = x_ref.shape[1] // 4
    width = wkg.shape[2]
    lbo = width // 128
    fe = dn_ref.shape[3]
    rows = nz * nx * 4
    i = lax.axis_index("rows")
    p = lax.axis_index("tp")
    y, c = i // CORES, i % CORES
    z, x = p // nx, p % nx
    far = nz // 2

    def step(q):
        return far + (1 - 2 * (q % 2)) * ((q + 1) // 2)

    def to_z(q):
        return (z + step(q)) % nz

    hops = TURNS[nz]

    def at_x(k):
        return (x + k) % nx

    def z_dev(zz):
        return (i, zz * nx + x)

    def x_dev(xx):
        return (i, z * nx + xx)

    def r_dev(ii):
        return (ii, p)

    other = r_dev(y * CORES + 1 - c)

    def send(src, dst, ss_, rs_, dev):
        return pltpu.make_async_remote_copy(
            src_ref=src, dst_ref=dst, send_sem=ss_, recv_sem=rs_, device_id=dev, device_id_type=MESH
        )

    def turns(body):
        def one(q, t):
            body(q)
            return t

        lax.fori_loop(0, nz - 1, one, 0)

    barrier = pltpu.get_barrier_semaphore()
    turns(lambda q: pl.semaphore_signal(barrier, inc=1, device_id=z_dev(to_z(q)), device_id_type=MESH))
    for k in range(1, nr):
        pl.semaphore_signal(barrier, inc=1, device_id=r_dev((i + k) % nr), device_id_type=MESH)
    for k in range(1, nx):
        pl.semaphore_signal(barrier, inc=1, device_id=x_dev(at_x(k)), device_id_type=MESH)

    x_own = pltpu.make_async_copy(x_ref.at[z], xg.at[x, z], loc.at[0])
    d_own = pltpu.make_async_copy(dn_ref.at[i], dsp.at[pl.ds(2 * i, 2)], loc.at[1])
    w_own = (
        pltpu.make_async_copy(wk_ref, wkg.at[x], loc.at[2]),
        pltpu.make_async_copy(wv_ref, wvg.at[x], loc.at[3]),
        pltpu.make_async_copy(up_ref, ug.at[x], loc.at[4]),
    )
    for one in (x_own, d_own) + w_own:
        one.start()

    pl.semaphore_wait(barrier, nr + nx + nz - 3)

    def xz_copy(q):
        return send(x_ref.at[to_z(q)], xg.at[x, z], xz_s.at[q], xz_r.at[q], z_dev(to_z(q)))

    def dr_copy(k):
        to = (i + k) % nr
        return send(dn_ref.at[to], dsp.at[pl.ds(2 * i, 2)], dr_s.at[k], dr_r.at[k], r_dev(to))

    for k in range(1, nr):
        dr_copy(k).start()
    turns(lambda q: xz_copy(q).start())

    deep = wk_ref.shape[0]

    def share(n):
        return pl.ds(pl.multiple_of(c * (n // CORES), n // CORES), n // CORES)

    def wk_copy(k, h):
        few = deep // (2 * CORES)
        some = pl.ds(pl.multiple_of(c * (deep // CORES) + h * few, few), few)
        return send(wk_ref.at[some], wkg.at[x, some], wk_s.at[k, h], wk_r.at[k, h], x_dev(at_x(k)))

    def wv_copy(k):
        some = share(deep)
        return send(wv_ref.at[some], wvg.at[x, some], wv_s.at[k], wv_r.at[k], x_dev(at_x(k)))

    def up_copy(k):
        some = share(RANK)
        return send(up_ref.at[some], ug.at[x, some], up_s.at[k], up_r.at[k], x_dev(at_x(k)))

    def pass_on(ref, n, s_sem, r_sem, k):
        xx, some = (x + nx - k) % nx, share(n)
        return send(ref.at[xx, some], ref.at[xx, some], s_sem.at[k], r_sem.at[k], other)

    def wkc_copy(k):
        return pass_on(wkg, deep, wkc_s, wkc_r, k)

    def wvc_copy(k):
        return pass_on(wvg, deep, wvc_s, wvc_r, k)

    def upc_copy(k):
        return pass_on(ug, RANK, upc_s, upc_r, k)

    for k in range(1, nx):
        wk_copy(k, 0).start()
        up_copy(k).start()

    group = rows // 2
    ids = jnp.broadcast_to(id_ref[...].astype(F32).astype(BF16), (8, group))
    r_a = lax.broadcasted_iota(jnp.int32, (group, rows), 0)
    n_a = lax.broadcasted_iota(jnp.int32, (group, rows), 1)
    idr = dot(ids, (r_a == (n_a >> 2) * 2 + (n_a & 1)).astype(F32).astype(BF16))[:1].astype(jnp.int32)
    r_b = lax.broadcasted_iota(jnp.int32, (rows, group), 1)
    n_b = lax.broadcasted_iota(jnp.int32, (rows, group), 0)
    idc = dot_t((r_b == (n_b >> 2) * 2 + (n_b & 1)).astype(F32).astype(BF16), ids)[:, :1].astype(jnp.int32)

    bits_x, bits_lb = log2(nx), log2(lbs)
    rho_r = lax.broadcasted_iota(jnp.int32, (rows, rows), 1)
    rho_c = lax.broadcasted_iota(jnp.int32, (rows, rows), 0)
    same = (idr == idc) & (((rho_r ^ rho_c) & 2) == 0)
    slot_r = jnp.sum((same & (rho_c < rho_r)).astype(F32), axis=0, keepdims=True).astype(jnp.int32)
    slot_c = jnp.sum((same & (rho_r < rho_c)).astype(F32), axis=1, keepdims=True).astype(jnp.int32)
    half = qg * SLOTS
    slots = 2 * nz * SLOTS
    sig = lax.broadcasted_iota(jnp.int32, (slots, rows), 0)
    rho = lax.broadcasted_iota(jnp.int32, (slots, rows), 1)
    t_sig = (sig >> log2(half)) & 1
    col_sig = lax.broadcasted_iota(jnp.int32, (slots, 1), 0)
    q_sig = (col_sig >> log2(2 * half)) * qg + ((col_sig & (half - 1)) >> 3)
    za_sig = jnp.zeros((slots, 1), jnp.int32)
    for q in range(nz):
        za_sig = jnp.where(q_sig == q, (z + nz - hops[q]) % nz, za_sig)
    gather = (
        (idr == za_sig * nx + x) & (slot_r == (sig & (SLOTS - 1))) & (((rho >> 1) & 1) == t_sig)
    ).astype(F32).astype(BF16)
    spot = lax.broadcasted_iota(jnp.int32, (rows, nx * SLOTS), 1)
    place = (
        (idc == z * nx + (spot >> 3)) & (slot_c == (spot & (SLOTS - 1)))
    ).astype(F32).astype(BF16)

    block = 2 * nx * 4 * lbs
    o = lax.broadcasted_iota(jnp.int32, (block, block), 0)
    n = lax.broadcasted_iota(jnp.int32, (block, block), 1)
    r_o = o & 3
    x_o = (o >> 2) & (nx - 1)
    z_o = (o >> (2 + bits_x)) & 1
    l_o = o >> (3 + bits_x)
    perm = (n == ((((x_o * 2 + z_o) * 4 + r_o) << bits_lb) + l_o)).astype(F32).astype(BF16)

    tail = nz * 4
    o_own = lax.broadcasted_iota(jnp.int32, (tail, rows), 0)
    n_own = lax.broadcasted_iota(jnp.int32, (tail, rows), 1)
    own = (n_own == (o_own >> 2) * (4 * nx) + 4 * x + (o_own & 3)).astype(F32).astype(BF16)
    place = dot(own, place)
    big = tail * lbo
    o_out = lax.broadcasted_iota(jnp.int32, (big, big), 0)
    n_out = lax.broadcasted_iota(jnp.int32, (big, big), 1)
    spread = (
        n_out == (o_out & (lbo - 1)) * tail + (o_out >> log2(lbo))
    ).astype(F32).astype(BF16)

    def parcels(part):
        tall = jnp.concatenate([part[:, lb * 128:(lb + 1) * 128] for lb in range(lbo)], axis=0)
        return dot(spread, tall).astype(BF16).reshape(nz, 4 * lbo, 128)

    for k in range(1, nr):
        dr_copy(k).wait_recv()
    d_own.wait()

    def dz_copy(q):
        to = (z + hops[q]) % nz
        return send(dsp.at[to], dg.at[i, q], dz_s.at[q], dz_r.at[q], z_dev(to))

    def over_z(g):
        if g > 1:
            for q in range((g - 2) * qg, (g - 1) * qg):
                if hops[q]:
                    dz_copy(q).wait_send()
        for q in range(g * qg, (g + 1) * qg):
            if hops[q]:
                dz_copy(q).start()

    over_z(0)
    over_z(1)
    e_own = pltpu.make_async_copy(dsp.at[z], dg.at[i, hops.index(0)], loc.at[5])
    e_own.start()

    turns(lambda q: xz_copy(q).wait_recv())
    x_own.wait()

    def xx_copy(k):
        return send(xg.at[x], xg.at[x], xx_s.at[k], xx_r.at[k], x_dev(at_x(k)))

    for k in range(1, nx):
        xx_copy(k).start()

    def dy_copy(j, g):
        some = pl.ds(g * qg, qg)
        to = ((y + j) % ny) * CORES + c
        return send(dg.at[i, some], dg.at[i, some], dy_s.at[j, g], dy_r.at[j, g], r_dev(to))

    def dc_copy(j, g):
        some = pl.ds(g * qg, qg)
        e = ((y + ny - j) % ny) * CORES + c
        return send(dg.at[e, some], dg.at[e, some], dc_s.at[j, g], dc_r.at[j, g], other)

    def over_y(g):
        for q in range(g * qg, (g + 1) * qg):
            if hops[q]:
                dz_copy(q).wait_recv()
            else:
                e_own.wait()
        for j in range(1, ny):
            dy_copy(j, g).start()
        dc_copy(0, g).start()

    def over_core(g):
        for j in range(1, ny):
            dy_copy(j, g).wait_recv()
            dc_copy(j, g).start()

    def s_copy(q):
        return send(ss.at[q], sr.at[q], s_s.at[q], s_r.at[q], z_dev((z + nz - hops[q]) % nz))

    def shrink(g, picked):
        for j in range(ny):
            dc_copy(j, g).wait_recv()
        acc = jnp.zeros((2 * half, qg * RANK), F32)
        for e in range(0, nr, 2):
            block_d = jnp.concatenate(
                [dg[e + b, g * qg:(g + 1) * qg].reshape(qg * RANK, fe) for b in range(2)], axis=1
            )
            acc = acc + dot_t(picked[2 * half * g:2 * half * (g + 1), e * fe:(e + 2) * fe], block_d)
        for a in range(qg):
            first = acc[a * SLOTS:(a + 1) * SLOTS, a * RANK:(a + 1) * RANK]
            second = acc[half + a * SLOTS:half + (a + 1) * SLOTS, a * RANK:(a + 1) * RANK]
            q = g * qg + a
            if hops[q]:
                ss[q] = jnp.concatenate([first, second], axis=1)
                s_copy(q).start()
            else:
                sr[q] = jnp.concatenate([first, second], axis=1)

    def k_copy(q):
        return send(ks.at[to_z(q)], kr.at[q], k_s.at[q], k_r.at[q], z_dev(to_z(q)))

    for g in range(2, ng):
        over_z(g)
    over_y(0)

    for k in range(1, nx):
        xx_copy(k).wait_recv()
    for k in range(1, nx):
        wk_copy(k, 1).start()
    for k in range(1, nx):
        wv_copy(k).start()
    zb = nz // 2
    wide = jnp.concatenate(
        [xg[:, 2 * b:2 * b + 2].reshape(block, 128) for b in range(zb)], axis=1
    )
    turned = dot(perm, wide).astype(BF16)
    tall = 8 * nx
    for b in range(zb):
        for lb in range(lbs):
            xm[b * tall:(b + 1) * tall, lb * 128:(lb + 1) * 128] = turned[
                lb * tall:(lb + 1) * tall, b * 128:(b + 1) * 128
            ]
    picked = dot(gather, xm[...]).astype(BF16)

    for g in range(1, ng):
        over_y(g)
        if g > 1:
            over_core(g - 2)
    over_core(ng - 2)
    for g in range(ng - 2):
        shrink(g, picked)
    over_core(ng - 1)
    shrink(ng - 2, picked)
    shrink(ng - 1, picked)

    for k in range(1, nx):
        for h in range(2):
            wk_copy(k, h).wait_recv()
        wkc_copy(k).start()
    x_rows = dot(own, xm[...]).astype(BF16)
    for one in w_own:
        one.wait()
    for k in range(1, nx):
        wkc_copy(k).wait_recv()
    ks[...] = parcels(dot(x_rows, wkg[...].reshape(nx * deep, width)).astype(BF16))
    turns(lambda q: k_copy(q).start())
    kr[nz - 1] = ks[z]

    for k in range(1, nx):
        up_copy(k).wait_recv()
        upc_copy(k).start()
    for q in range(nz):
        if hops[q]:
            s_copy(q).wait_recv()
    sh[x] = jnp.sum(sr[...], axis=0).astype(BF16).astype(F32)

    def sh_copy(k):
        return send(sh.at[x], sh.at[x], sh_s.at[k], sh_r.at[k], x_dev(at_x(k)))

    for k in range(1, nx):
        sh_copy(k).start()
    for k in range(1, nx):
        wv_copy(k).wait_recv()
        wvc_copy(k).start()
    for k in range(1, nx):
        wvc_copy(k).wait_recv()
        upc_copy(k).wait_recv()
    vp = dot(x_rows, wvg[...].reshape(nx * deep, width))
    lane = lax.broadcasted_iota(jnp.int32, (tail, 2 * RANK), 1)
    row_l = lax.broadcasted_iota(jnp.int32, (tail, 2 * RANK), 0)
    mine = ((row_l >> 1) & 1) == (lane >= RANK).astype(jnp.int32)
    spot_o = lax.broadcasted_iota(jnp.int32, (tail, nx * SLOTS), 1) >> 3
    places = [jnp.where(spot_o == xa, place, 0.0).astype(BF16) for xa in range(nx)]
    for k in range(1, nx):
        sh_copy(k).wait_recv()
    shrinks = sh[...].reshape(nx * SLOTS, 2 * RANK).astype(BF16)
    lows = []
    for xa in range(nx):
        low_a = jnp.where(mine, dot(places[xa], shrinks), 0.0)
        lows.append(low_a + jnp.concatenate([low_a[:, RANK:], low_a[:, :RANK]], axis=1))
    low = jnp.concatenate(
        [jnp.where(lane < RANK, lows[xa], lows[xa + 1]) for xa in range(0, nx, 2)], axis=1
    ).astype(BF16)
    vp = vp + dot(low, ug[...].reshape(nx * RANK, width))
    vs[...] = parcels(vp.astype(BF16))

    def v_copy(q):
        return send(vs.at[to_z(q)], vr.at[q], v_s.at[q], v_r.at[q], z_dev(to_z(q)))

    turns(lambda q: v_copy(q).start())
    vr[nz - 1] = vs[z]
    turns(lambda q: k_copy(q).wait_recv())
    ko_ref[...] = jnp.sum(kr[...].astype(F32), axis=0).astype(BF16)

    for k in range(1, nr):
        dr_copy(k).wait_send()
    for k in range(1, nx):
        for h in range(2):
            wk_copy(k, h).wait_send()
        for one in (wv_copy, up_copy, wkc_copy, wvc_copy, upc_copy):
            one(k).wait_send()
        xx_copy(k).wait_send()
        sh_copy(k).wait_send()
    for g in range(ng):
        for j in range(1, ny):
            dy_copy(j, g).wait_send()
        for j in range(ny):
            dc_copy(j, g).wait_send()

    def left(q):
        xz_copy(q).wait_send()
        k_copy(q).wait_send()

    turns(left)
    for q in range(nz):
        if hops[q]:
            s_copy(q).wait_send()
            if q >= (ng - 2) * qg:
                dz_copy(q).wait_send()

    turns(lambda q: v_copy(q).wait_recv())
    vo_ref[...] = jnp.sum(vr[...].astype(F32), axis=0).astype(BF16)
    turns(lambda q: v_copy(q).wait_send())


def shards(nr, nz, nx, hidden, adapter_ids, key_weight, value_weight, adapter_down, adapter_up):
    steps, own, wide = hidden.shape
    width = key_weight.shape[1]
    lbo = width // 128
    deep = key_weight.shape[0]
    fz = wide // nz
    lbs = fz // 128
    fe = fz // nr
    rows = nz * nx * 4
    xz = hidden.reshape(4, nz, lbs, 128).transpose(1, 0, 2, 3).reshape(nz, 4 * lbs, 128)
    dn = adapter_down.reshape(2, nr, fe, RANK).transpose(1, 0, 3, 2)
    any_, vmem = pl.BlockSpec(memory_space=pl.ANY), pl.BlockSpec(memory_space=pltpu.VMEM)
    dma = pltpu.SemaphoreType.DMA
    ng = 4 if nz >= 16 else 2
    ny = nr // CORES
    key_out, value_out = pl.pallas_call(
        functools.partial(kernel, nr, nz, nx, ng),
        out_shape=[jax.ShapeDtypeStruct((4 * lbo, 128), BF16)] * 2,
        in_specs=[any_, vmem, any_, any_, any_, any_],
        out_specs=[vmem, vmem],
        scratch_shapes=[
            pltpu.VMEM((nx, nz, 4 * lbs, 128), BF16),
            pltpu.VMEM((nx, deep, width), BF16),
            pltpu.VMEM((nx, deep, width), BF16),
            pltpu.VMEM((nx, RANK, width), BF16),
            pltpu.VMEM((nz, RANK, fe), BF16),
            pltpu.VMEM((nr, nz, RANK, fe), BF16),
            pltpu.VMEM((rows, fz), BF16),
            pltpu.VMEM((nz, SLOTS, 2 * RANK), F32),
            pltpu.VMEM((nz, SLOTS, 2 * RANK), F32),
            pltpu.VMEM((nx, SLOTS, 2 * RANK), F32),
            pltpu.VMEM((nz, 4 * lbo, 128), BF16),
            pltpu.VMEM((nz, 4 * lbo, 128), BF16),
            pltpu.VMEM((nz, 4 * lbo, 128), BF16),
            pltpu.VMEM((nz, 4 * lbo, 128), BF16),
            dma((6,)),
            dma((nz,)), dma((nz,)), dma((nx,)), dma((nx,)),
            dma((nx, 2)), dma((nx, 2)), dma((nx,)), dma((nx,)), dma((nx,)), dma((nx,)),
            dma((nx,)), dma((nx,)), dma((nx,)), dma((nx,)), dma((nx,)), dma((nx,)),
            dma((nr,)), dma((nr,)), dma((nz,)), dma((nz,)),
            dma((ny, ng)), dma((ny, ng)), dma((ny, ng)), dma((ny, ng)),
            dma((nz,)), dma((nz,)), dma((nx,)), dma((nx,)),
            dma((nz,)), dma((nz,)), dma((nz,)), dma((nz,)),
        ],
        compiler_params=pltpu.CompilerParams(
            collective_id=0, has_side_effects=True, vmem_limit_bytes=32 * 1024 * 1024
        ),
        cost_estimate=pl.CostEstimate(flops=2_000_000_000, bytes_accessed=4_000_000, transcendentals=0),
    )(xz, adapter_ids.reshape(1, rows // 2), key_weight, value_weight, dn, adapter_up[0])
    return key_out.reshape(steps, own, -1), value_out.reshape(steps, own, -1)


def solution(mesh):
    nr, tp = mesh.shape["rows"], mesh.shape["tp"]
    nx = 4 if tp >= 64 else 2
    placed = (
        P(None, ("rows", "tp"), None),
        P("rows", None),
        P("tp", None),
        P("tp", None),
        P("rows", "tp"),
        P("tp", None, None),
    )
    return jax.shard_map(
        functools.partial(shards, nr, tp // nx, nx),
        mesh=mesh,
        in_specs=placed,
        out_specs=(P(None, ("rows", "tp"), None), P(None, ("rows", "tp"), None)),
        check_vma=False,
    )
```
